256 devices in a mesh: dp: 64 (over z, y, core), group: 4 (over x).
Axes of the slice: x: 4, y: 4, z: 8, core: 2. Of those that a mesh axis runs over, the one named last changes fastest.
Arguments:
- tokens: bfloat16 [262144, 512], P(('dp', 'group'))
- stamps: int32 [262144], P(('dp', 'group')), may hold values from 0 to 523776, as said below
- lengths: int32 [64, 4, 4], P('dp', 'group'), may hold values from 1 to 768, as said below
- in_weight: bfloat16 [512, 2048], P(None, ('dp', 'group')), may hold values from -0.25 to 0.25
- out_weight: bfloat16 [512, 512], P(None, 'dp'), may hold values from -0.25 to 0.25
- pos_table: float32 [12], replicated, may hold values from -1.5 to 1.5
- time_table: float32 [20], replicated, may hold values from -1.5 to 1.5
Outputs:
- updated: bfloat16 [262144, 512], P(('dp', 'group'))
The draws below stay inside these ranges and needn't reach their ends.
Inputs may be any that keep to these rules, and one draw needn't show every extreme that they name: Each device's 4 lengths sum to 1024. The longest history of a device grows with its dp index, from about 1024 / 4 rows at index 0; every device at the last dp index holds one of 768 rows. `stamps`: within each device's 1024 rows the times never fall, the first row's time is 0 and the last row's time is 523776.
All inputs are finite; a program needn't handle non-finite values.
Results may differ from the reference program's by a relative error of at most 0.0055.
Values may be sent and summed in bfloat16 or wider, within the bound.
No kernel may reach another device: no remote copies, remote signals or barrier semaphores. Data moves between devices by JAX's collectives and lax.ppermute only.
A program may use at most 64 MiB of HBM per device.

```python
import math
import jax
import jax.numpy as jnp
from jax import lax

D = 512
HEADS = 4
HEAD_DIM = 128
TOK_DEV = 1024
SEQ_DEV = 4
QBLOCK = 512
POS_BUCKETS = 12
TIME_BUCKETS = 20
LONGEST = 768
ROWS = 262144
N_DP = 64
N_GROUP = 4


def draw_tokens(key, part):
    key = jax.random.fold_in(key, 11)
    scale_key, value_key = jax.random.split(key)
    column_scale = jnp.exp(jax.random.uniform(scale_key, (1, D), jnp.float32, math.log(0.3), math.log(3.0)))
    values = jax.random.normal(value_key, (ROWS, D), jnp.float32)
    return (values * column_scale).astype(jnp.bfloat16)


def draw_stamps(key, part):
    key = jax.random.fold_in(key, 23)
    power_key, gap_key = jax.random.split(key)
    exponent = jax.random.randint(power_key, (ROWS,), 0, 10)
    gaps = jax.random.randint(gap_key, (ROWS,), 0, jnp.left_shift(1, exponent))
    gaps = gaps.reshape(ROWS // TOK_DEV, TOK_DEV)
    times_all = jnp.cumsum(gaps, axis=1) - gaps
    final_time = jnp.full((ROWS // TOK_DEV, 1), 512 * (TOK_DEV - 1), jnp.int32)
    times_all = jnp.concatenate([times_all[:, :-1].astype(jnp.int32), final_time], axis=1)
    return times_all.reshape(ROWS).astype(jnp.int32)


def draw_lengths(key, part):
    key = jax.random.fold_in(key, 37)
    shrink_key, order_key = jax.random.split(key)
    short_length = TOK_DEV // SEQ_DEV
    dp_index = jnp.arange(N_DP, dtype=jnp.int32)[:, None, None]
    longest = short_length + (LONGEST - short_length) * dp_index // max(N_DP - 1, 1)
    longest = jnp.broadcast_to(longest, (N_DP, N_GROUP, 1))
    remain = TOK_DEV - longest
    base_length = remain // (SEQ_DEV - 1)
    shrink = jax.random.randint(shrink_key, (N_DP, N_GROUP, SEQ_DEV - 2), 0, base_length // 4 + 1)
    middle = base_length - shrink
    last_length = remain - jnp.sum(middle, axis=-1, keepdims=True)
    lengths_all = jnp.concatenate([longest, middle, last_length], axis=-1)
    scores = jax.random.randint(order_key, (N_DP, N_GROUP, SEQ_DEV), 0, 1024) * SEQ_DEV + jnp.arange(SEQ_DEV, dtype=jnp.int32)
    ordering = jnp.argsort(scores, axis=-1)
    return jnp.take_along_axis(lengths_all, ordering, axis=-1).astype(jnp.int32)


def steps_of(own_key, shape, shards, smallest, largest):
    level = 1.0
    for axis_at, shards_of in shards:
        draws = jax.random.uniform(jax.random.fold_in(jax.random.fold_in(own_key, 6), axis_at), (shards_of,), jnp.float32, smallest / len(shards), largest / len(shards))
        level = level * jnp.repeat(jnp.exp(draws), shape[axis_at] // shards_of).reshape((-1,) + (1,) * (len(shape) - 1 - axis_at))
    return level


def centred(stream_key, extent, scale, most, cuts=(), held_as=jnp.bfloat16):
    loudness = steps_of(stream_key, extent, cuts, -0.22, 0.18) if cuts else 1.0
    entries = jax.random.normal(stream_key, extent, jnp.float32) * scale * loudness
    return jnp.minimum(jnp.maximum(entries, -most), most).astype(held_as)


def setup_inputs(seed: int = 0) -> dict:
    streams_of = jax.random.split(jax.random.key(seed), 8)
    tokens = draw_tokens(jax.random.fold_in(streams_of[7], 71), 0)
    stamps = draw_stamps(jax.random.fold_in(streams_of[7], 71), 0)
    lengths = draw_lengths(jax.random.fold_in(streams_of[7], 71), 0)
    in_weight = centred(streams_of[3], (D, 4 * D), D ** -0.5, 0.25, ((1, 256),))
    out_weight = centred(streams_of[4], (D, D), D ** -0.5, 0.25, ((1, 64),))
    pos_table = jnp.clip(jax.random.uniform(streams_of[5], (POS_BUCKETS,), jnp.float32, -1.5, 1.5), -1.5, 1.5)
    time_table = jnp.clip(jax.random.uniform(streams_of[6], (TIME_BUCKETS,), jnp.float32, -1.5, 1.5), -1.5, 1.5)
    return dict(tokens=tokens, stamps=stamps, lengths=lengths, in_weight=in_weight, out_weight=out_weight, pos_table=pos_table, time_table=time_table)


def layer_norm(values):
    center = values - lax.optimization_barrier(jnp.mean(values, axis=-1, keepdims=True))
    spread = lax.optimization_barrier(jnp.mean(center * center, axis=-1, keepdims=True))
    return center * lax.rsqrt(spread + 1e-05)

def bucket_ids(gap, count):
    total = jnp.zeros(gap.shape, jnp.int32)
    for power in range(1, count):
        total = total + (gap + 1 >= 2 ** power).astype(jnp.int32)
    return total

def table_bias(ids, table, count):
    result = jnp.zeros(ids.shape, jnp.float32)
    for entry in range(count):
        result = result + jnp.where(ids == entry, table[entry], 0.0)
    return result

def row_layout(lengths, count):
    ends = jnp.cumsum(lengths).astype(jnp.int32)
    starts = (ends - lengths).astype(jnp.int32)
    row_ids = jnp.arange(count, dtype=jnp.int32)
    segment = lax.optimization_barrier(jnp.sum((row_ids[:, None] >= ends[None, :]).astype(jnp.int32), axis=1)).astype(jnp.int32)
    slots = jnp.arange(lengths.shape[0], dtype=jnp.int32)
    first_row = lax.optimization_barrier(jnp.sum(jnp.where(segment[:, None] == slots[None, :], starts[None, :], 0), axis=1)).astype(jnp.int32)
    return (segment, first_row)

def attend_block(value_part, query_part, key_part, segment, first_row, stamp_rows, pos_table, time_table, block_index):
    width = QBLOCK
    scale = HEAD_DIM ** (-0.5)
    row_start = block_index * width
    query_rows = lax.dynamic_slice_in_dim(query_part, row_start, width, 0).reshape(width, HEADS, HEAD_DIM).astype(jnp.float32)
    query_seg = lax.dynamic_slice_in_dim(segment, row_start, width, 0)
    query_stamp = lax.dynamic_slice_in_dim(stamp_rows, row_start, width, 0)
    query_index = row_start + jnp.arange(width, dtype=jnp.int32)
    low_tile = lax.dynamic_index_in_dim(first_row, row_start, keepdims=False) // width

    def tile_step(tile_index, totals):
        col_start = tile_index * width
        key_rows = lax.dynamic_slice_in_dim(key_part, col_start, width, 0).reshape(width, HEADS, HEAD_DIM).astype(jnp.float32)
        value_rows = lax.dynamic_slice_in_dim(value_part, col_start, width, 0).reshape(width, HEADS, HEAD_DIM).astype(jnp.float32)
        key_seg = lax.dynamic_slice_in_dim(segment, col_start, width, 0)
        key_stamp = lax.dynamic_slice_in_dim(stamp_rows, col_start, width, 0)
        key_index = col_start + jnp.arange(width, dtype=jnp.int32)
        scores = jnp.einsum('qhd,khd->hqk', query_rows, key_rows) * scale
        offset = query_index[:, None] - key_index[None, :]
        elapsed = query_stamp[:, None] - key_stamp[None, :]
        bias = table_bias(bucket_ids(offset, POS_BUCKETS), pos_table, POS_BUCKETS) + table_bias(bucket_ids(elapsed, TIME_BUCKETS), time_table, TIME_BUCKETS)
        live = (query_seg[:, None] == key_seg[None, :]) & (offset >= 0)
        weights = jnp.where(live[None], jax.nn.silu(scores + bias[None]), 0.0).astype(jnp.bfloat16)
        weights = lax.optimization_barrier(weights).astype(jnp.float32)
        return totals + jnp.einsum('hqk,khd->qhd', weights, value_rows)
    totals = lax.fori_loop(low_tile, block_index + 1, tile_step, jnp.zeros((width, HEADS, HEAD_DIM), jnp.float32))
    return totals.reshape(width, HEADS * HEAD_DIM).astype(jnp.bfloat16)

def one_buffer(inputs, in_weight, out_weight, pos_table, time_table):
    rows_in, stamp_rows, buffer_lengths = inputs
    normed = layer_norm(rows_in.astype(jnp.float32)).astype(jnp.bfloat16)
    mixed = jax.nn.silu(jnp.dot(normed, in_weight, preferred_element_type=jnp.float32)).astype(jnp.bfloat16)
    segment, first_row = row_layout(buffer_lengths, TOK_DEV)
    value_part = mixed[:, D:2 * D]
    query_part = mixed[:, 2 * D:3 * D]
    key_part = mixed[:, 3 * D:]
    pieces = [attend_block(value_part, query_part, key_part, segment, first_row, stamp_rows, pos_table, time_table, index) for index in range(TOK_DEV // QBLOCK)]
    attended = jnp.concatenate(pieces, axis=0)
    gated = (layer_norm(attended.astype(jnp.float32)) * mixed[:, :D].astype(jnp.float32)).astype(jnp.bfloat16)
    return (rows_in.astype(jnp.float32) + jnp.dot(gated, out_weight, preferred_element_type=jnp.float32)).astype(jnp.bfloat16)

def reference(tokens, stamps, lengths, in_weight, out_weight, pos_table, time_table):
    buffers = N_DP * N_GROUP
    token_all = tokens.reshape(buffers, TOK_DEV, D)
    stamp_all = stamps.reshape(buffers, TOK_DEV)
    length_all = lengths.reshape(buffers, SEQ_DEV)
    result = lax.map(lambda inputs: one_buffer(inputs, in_weight, out_weight, pos_table, time_table), (token_all, stamp_all, length_all))
    return result.reshape(ROWS, D)
```

```python
import functools

import jax
import jax.numpy as jnp
from jax import lax
from jax.experimental import pallas as pl
from jax.experimental.pallas import tpu as pltpu
from jax.sharding import PartitionSpec as P

D = 512
HEADS = 4
HEAD_DIM = 128
ROWS = 1024
BLOCK = 256
TILE = 128
POS_BUCKETS = 12
TIME_BUCKETS = 20
NEVER = -1e30
TRANS_B = (((1,), (1,)), ((), ()))
PAIRS = [(i, j) for i in range(ROWS // BLOCK) for j in range(i + 1)]


def normalize(values):
    center = values - jnp.mean(values, axis=-1, keepdims=True)
    spread = jnp.mean(center * center, axis=-1, keepdims=True)
    return center * lax.rsqrt(spread + 1e-05)


def prepare_kernel(lengths, pos_table, time_table, tokens, stamps, normed, bias, pos_tiles):
    for i in range(ROWS // BLOCK):
        rows = slice(i * BLOCK, (i + 1) * BLOCK)
        normed[rows, :] = normalize(tokens[rows, :].astype(jnp.float32)).astype(jnp.bfloat16)

    apart = lax.broadcasted_iota(jnp.int32, (TILE, TILE), 0) - lax.broadcasted_iota(
        jnp.int32, (TILE, TILE), 1
    )
    for d in range(ROWS // TILE):
        offset = apart + d * TILE
        tile = jnp.full((TILE, TILE), pos_table[0] * 0.5, jnp.float32)
        for power in range(1, POS_BUCKETS):
            if 2**power - 1 <= (d + 1) * TILE - 1:
                tile = jnp.where(offset + 1 >= 2**power, pos_table[power] * 0.5, tile)
        pos_tiles[d] = jnp.where(offset >= 0, tile, NEVER)

    first = lengths[0]
    second = first + lengths[1]
    third = second + lengths[2]
    row_id = (
        lax.broadcasted_iota(jnp.int32, (8, TILE), 0) * TILE
        + lax.broadcasted_iota(jnp.int32, (8, TILE), 1)
    )
    segment = (
        (row_id >= first).astype(jnp.int32)
        + (row_id >= second).astype(jnp.int32)
        + (row_id >= third).astype(jnp.int32)
    )
    times = stamps[...] + segment * (1 << 20)

    lane = lax.broadcasted_iota(jnp.int32, (TILE, TILE), 1)
    lookup = jnp.full((TILE, TILE), NEVER, jnp.float32)
    for entry in range(TIME_BUCKETS):
        lookup = jnp.where(lane == 31 - entry, time_table[entry] * 0.5, lookup)

    for i in range(ROWS // TILE):
        own = jnp.transpose(jnp.broadcast_to(times[i : i + 1, :], (TILE, TILE)))
        own = own + 1
        for j in range(ROWS // TILE):
            qi, kj = i // 2, j // 2
            if kj > qi:
                continue
            at = PAIRS.index((qi, kj))
            rows, cols = pl.ds((i % 2) * TILE, TILE), pl.ds((j % 2) * TILE, TILE)
            if j > i:
                bias[at, rows, cols] = jnp.full((TILE, TILE), NEVER, jnp.float32)
                continue
            gap = own - times[j : j + 1, :]
            time_bias = jnp.take_along_axis(lookup, lax.clz(gap), axis=1)
            bias[at, rows, cols] = time_bias + pos_tiles[i - j]


def prepare(lengths, pos_table, time_table, tokens, stamps):
    smem = pl.BlockSpec(memory_space=pltpu.SMEM)
    vmem = pl.BlockSpec(memory_space=pltpu.VMEM)
    return pl.pallas_call(
        prepare_kernel,
        out_shape=(
            jax.ShapeDtypeStruct((ROWS, D), jnp.bfloat16),
            jax.ShapeDtypeStruct((len(PAIRS), BLOCK, BLOCK), jnp.float32),
        ),
        in_specs=[smem, smem, smem, vmem, vmem],
        out_specs=(vmem, vmem),
        scratch_shapes=[pltpu.VMEM((ROWS // TILE, TILE, TILE), jnp.float32)],
        compiler_params=pltpu.CompilerParams(vmem_limit_bytes=40 * 2**20),
        cost_estimate=pl.CostEstimate(flops=2 * 10**7, bytes_accessed=5 * 10**6, transcendentals=0),
    )(lengths, pos_table, time_table, tokens, stamps)


def half_silu(z):
    return z + z * jnp.tanh(z)


def main_kernel(
    lengths, tokens_hbm, normed_hbm, bias_hbm, *refs
):
    planes_hbm, updated_hbm = refs[:8], refs[8]
    (
        tokens, normed, bias, planes, in_weight, out_weight, mixed, totals, updated, sems, out_sems,
    ) = refs[9:]
    dp, own_x = lax.axis_index("dp"), lax.axis_index("group")
    own_m, own_y, own_core = dp // 16, lax.rem(dp // 2, 4), lax.rem(dp, 2)
    def fetch(k, source, target):
        copy = pltpu.make_async_copy(source, target, sems.at[k])
        copy.start()
        return copy

    copy_normed = fetch(0, normed_hbm, normed)
    copies_in = []
    for side in range(2):
        core = own_core if side == 0 else 1 - own_core
        place = jnp.where(core == 0, own_y, own_x)
        for k in range(4):
            copies_in.append(
                fetch(
                    3 + side * 4 + k,
                    planes_hbm[side * 4 + k],
                    planes.at[core * 4 + lax.rem(place + 4 - k, 4)],
                )
            )
    copy_bias = fetch(1, bias_hbm, bias)
    copy_tokens = fetch(2, tokens_hbm, tokens)

    starts = [jnp.int32(0)]
    for k in range(3):
        starts.append(starts[-1] + lengths[k])

    copy_normed.wait()
    for copy in copies_in:
        copy.wait()

    def arrange(at, carry):
        m, y = at // 4, lax.rem(at, 4)
        m_slot = lax.rem(own_m + 4 - m, 4)
        units = []
        for core in range(2):
            for x in range(4):
                if core == 0:
                    plane, slot = y, lax.rem(own_x + 4 - x, 4)
                else:
                    plane, slot = 4 + x, lax.rem(own_y + 4 - y, 4)
                start = pl.multiple_of((slot * 4 + m_slot) * 16, 16)
                units.append(planes[plane, pl.ds(start, 16), :].astype(jnp.float32))
        for odd in range(2):
            halves = [unit[odd * 8 : odd * 8 + 8] for unit in units]
            start = pl.multiple_of(m * 512 + odd * 256 + y * 64, 64)
            in_weight[pl.ds(start, 64), :] = jnp.concatenate(
                [half[:, :D] for half in halves]
            ).astype(jnp.bfloat16)
            sides = [jnp.concatenate([h[:, D:] for h in halves[c * 4 : c * 4 + 4]], axis=1) for c in range(2)]
            start = pl.multiple_of(m * 128 + odd * 64 + y * 16, 16)
            out_weight[pl.ds(start, 16), :] = jnp.concatenate(sides).astype(jnp.bfloat16)
        return carry

    lax.fori_loop(0, 16, arrange, 0)
    sends = []
    for i in range(ROWS // BLOCK):
        rows = pl.ds(i * BLOCK, BLOCK)
        for part in range(4):
            cols = pl.ds(part * D, D)
            product = lax.dot_general(
                normed[rows, :], in_weight[cols, :], TRANS_B, preferred_element_type=jnp.float32
            )
            mixed[rows, cols] = half_silu(product * 0.5).astype(jnp.bfloat16)
        if i == 0:
            copy_bias.wait()
        low = jnp.int32(0)
        for k in range(1, 4):
            low = jnp.where(starts[k] <= i * BLOCK, starts[k], low)

        def attend(j, first, i=i, rows=rows):
            keys = pl.ds(j * BLOCK, BLOCK)
            pair_bias = bias[PAIRS.index((i, j))]
            for head in range(HEADS):
                cols = [pl.ds(part * D + head * HEAD_DIM, HEAD_DIM) for part in range(4)]
                scores = lax.dot_general(
                    mixed[rows, cols[2]], mixed[keys, cols[3]], TRANS_B,
                    preferred_element_type=jnp.float32,
                )
                weights = half_silu(scores * (0.5 * HEAD_DIM**-0.5) + pair_bias).astype(jnp.bfloat16)
                product = jnp.dot(weights, mixed[keys, cols[1]], preferred_element_type=jnp.float32)
                own = pl.ds(head * HEAD_DIM, HEAD_DIM)
                totals[:, own] = product if first else totals[:, own] + product

        attend(i, True)
        for j in range(i):
            pl.when(low < (j + 1) * BLOCK)(functools.partial(attend, j, False))
        attended = totals[...].astype(jnp.bfloat16).astype(jnp.float32)
        gate = mixed[rows, pl.ds(0, D)].astype(jnp.float32)
        gated = (normalize(attended) * gate).astype(jnp.bfloat16)
        if i == 0:
            copy_tokens.wait()
        projected = lax.dot_general(
            gated, out_weight[...], TRANS_B, preferred_element_type=jnp.float32
        )
        updated[rows, :] = (tokens[rows, :].astype(jnp.float32) + projected).astype(jnp.bfloat16)
        copy = pltpu.make_async_copy(updated.at[rows, :], updated_hbm.at[rows, :], out_sems.at[i])
        copy.start()
        sends.append(copy)
    for copy in sends:
        copy.wait()


def main(lengths, tokens, normed, bias, planes):
    anywhere = pl.BlockSpec(memory_space=pl.ANY)
    return pl.pallas_call(
        main_kernel,
        out_shape=jax.ShapeDtypeStruct((ROWS, D), jnp.bfloat16),
        in_specs=[pl.BlockSpec(memory_space=pltpu.SMEM)] + [anywhere] * 11,
        out_specs=anywhere,
        scratch_shapes=[
            pltpu.VMEM((ROWS, D), jnp.bfloat16),
            pltpu.VMEM((ROWS, D), jnp.bfloat16),
            pltpu.VMEM((len(PAIRS), BLOCK, BLOCK), jnp.float32),
            pltpu.VMEM((8, 256, 640), jnp.bfloat16),
            pltpu.VMEM((4 * D, D), jnp.bfloat16),
            pltpu.VMEM((D, D), jnp.bfloat16),
            pltpu.VMEM((ROWS, 4 * D), jnp.bfloat16),
            pltpu.VMEM((BLOCK, D), jnp.float32),
            pltpu.VMEM((ROWS, D), jnp.bfloat16),
            pltpu.SemaphoreType.DMA((11,)),
            pltpu.SemaphoreType.DMA((ROWS // BLOCK,)),
        ],
        compiler_params=pltpu.CompilerParams(vmem_limit_bytes=50 * 2**20),
        cost_estimate=pl.CostEstimate(
            flops=5 * 10**9, bytes_accessed=9 * 10**6, transcendentals=4 * 10**6
        ),
    )(lengths, tokens, normed, bias, *planes)


def device_of(x, y, z, core):
    return ((z % 8 * 4 + y % 4) * 2 + core % 2) * 4 + x % 4


def moves(step):
    return [
        (device_of(x, y, z, core), device_of(*step(x, y, z, core)))
        for z in range(8)
        for y in range(4)
        for core in range(2)
        for x in range(4)
    ]


def send(array, step):
    return lax.ppermute(array, ("dp", "group"), moves(step))


def gather(in_weight, out_weight):
    group = lax.axis_index("group")
    z = lax.axis_index("dp") // 8
    own = lax.dynamic_slice_in_dim(out_weight.T, group * HEAD_DIM, HEAD_DIM, axis=1)
    piece = jnp.concatenate([in_weight.T, own], axis=1)
    other = send(piece, lambda x, y, z, core: (x, y, z ^ 1, core))
    even = z % 2 == 0
    unit = jnp.concatenate([jnp.where(even, piece, other), jnp.where(even, other, piece)])
    units = [unit] + [
        send(unit, lambda x, y, z, core, k=k: (x, y, z + 2 * k, core)) for k in (1, 2, 3)
    ]
    line = jnp.concatenate(units)
    lines = [line] + [
        send(line, lambda x, y, z, core, k=k: (x + k * (1 - core), y + k * core, z, core))
        for k in (1, 2, 3)
    ]
    plane = jnp.concatenate(lines)
    planes = [plane] + [
        send(plane, lambda x, y, z, core, k=k: (x + k * core, y + k * (1 - core), z, core))
        for k in (1, 2, 3)
    ]
    return planes + [send(plane, lambda x, y, z, core: (x, y, z, core + 1)) for plane in planes]


def shards(tokens, stamps, lengths, in_weight, out_weight, pos_table, time_table):
    own_lengths = lengths.reshape(-1)
    normed, bias = prepare(own_lengths, pos_table, time_table, tokens, stamps.reshape(8, TILE))
    return main(own_lengths, tokens, normed, bias, gather(in_weight, out_weight))


def solution(mesh):
    return jax.shard_map(
        shards,
        mesh=mesh,
        in_specs=(
            P(("dp", "group"), None),
            P(("dp", "group")),
            P("dp", "group", None),
            P(None, ("dp", "group")),
            P(None, "dp"),
            P(),
            P(),
        ),
        out_specs=P(("dp", "group"), None),
        check_vma=False,
    )
```

```python
import jax
import jax.numpy as jnp
from jax import lax
from jax.experimental import pallas as pl
from jax.experimental.pallas import tpu as pltpu
from jax.sharding import PartitionSpec as P

D = 512
HEADS = 4
HEAD_DIM = 128
ROWS = 1024
BLOCK = 256
TILE = 128
POS_BUCKETS = 12
TIME_BUCKETS = 20
NEVER = -1e30
VMEM_PREPARE = 16
VMEM_MAIN = 32
TRANS_B = (((1,), (1,)), ((), ()))
PAIRS = [(i, j) for i in range(ROWS // BLOCK) for j in range(i + 1)]


def normalize(values):
    center = values - jnp.mean(values, axis=-1, keepdims=True)
    spread = jnp.mean(center * center, axis=-1, keepdims=True)
    return center * lax.rsqrt(spread + 1e-05)


def prepare_kernel(
    lengths_hbm, pos_hbm, time_hbm, tokens_hbm, stamps_hbm, tokens, normed, bias,
    lengths, pos_table, time_table, stamps, pos_tiles, sems,
):
    copies = [
        pltpu.make_async_copy(source, target, sems.at[k])
        for k, (source, target) in enumerate(
            [
                (lengths_hbm, lengths),
                (pos_hbm, pos_table),
                (time_hbm, time_table),
                (stamps_hbm, stamps),
                (tokens_hbm, tokens),
            ]
        )
    ]
    for copy in copies:
        copy.start()
    for copy in copies:
        copy.wait()
    for i in range(ROWS // BLOCK):
        rows = slice(i * BLOCK, (i + 1) * BLOCK)
        normed[rows, :] = normalize(tokens[rows, :].astype(jnp.float32)).astype(jnp.bfloat16)

    apart = lax.broadcasted_iota(jnp.int32, (TILE, TILE), 0) - lax.broadcasted_iota(
        jnp.int32, (TILE, TILE), 1
    )
    for d in range(ROWS // TILE):
        offset = apart + d * TILE
        tile = jnp.full((TILE, TILE), pos_table[0] * 0.5, jnp.float32)
        for power in range(1, POS_BUCKETS):
            if 2**power - 1 <= (d + 1) * TILE - 1:
                tile = jnp.where(offset + 1 >= 2**power, pos_table[power] * 0.5, tile)
        pos_tiles[d] = jnp.where(offset >= 0, tile, NEVER)

    first = lengths[0]
    second = first + lengths[1]
    third = second + lengths[2]
    row_id = (
        lax.broadcasted_iota(jnp.int32, (8, TILE), 0) * TILE
        + lax.broadcasted_iota(jnp.int32, (8, TILE), 1)
    )
    segment = (
        (row_id >= first).astype(jnp.int32)
        + (row_id >= second).astype(jnp.int32)
        + (row_id >= third).astype(jnp.int32)
    )
    times = stamps[...] + segment * (1 << 20)

    lane = lax.broadcasted_iota(jnp.int32, (TILE, TILE), 1)
    lookup = jnp.full((TILE, TILE), NEVER, jnp.float32)
    for entry in range(TIME_BUCKETS):
        lookup = jnp.where(lane == 31 - entry, time_table[entry] * 0.5, lookup)

    for i in range(ROWS // TILE):
        own = jnp.transpose(jnp.broadcast_to(times[i : i + 1, :], (TILE, TILE)))
        own = own + 1
        for j in range(ROWS // TILE):
            qi, kj = i // 2, j // 2
            if kj > qi:
                continue
            at = PAIRS.index((qi, kj))
            rows, cols = pl.ds((i % 2) * TILE, TILE), pl.ds((j % 2) * TILE, TILE)
            if j > i:
                bias[at, rows, cols] = jnp.full((TILE, TILE), NEVER, jnp.float32)
                continue
            gap = own - times[j : j + 1, :]
            time_bias = jnp.take_along_axis(lookup, lax.clz(gap), axis=1)
            bias[at, rows, cols] = time_bias + pos_tiles[i - j]


def prepare(lengths, pos_table, time_table, tokens, stamps):
    anywhere = pl.BlockSpec(memory_space=pl.ANY)
    vmem = pl.BlockSpec(memory_space=pltpu.VMEM)
    return pl.pallas_call(
        prepare_kernel,
        out_shape=(
            jax.ShapeDtypeStruct((ROWS, D), jnp.bfloat16),
            jax.ShapeDtypeStruct((ROWS, D), jnp.bfloat16),
            jax.ShapeDtypeStruct((len(PAIRS), BLOCK, BLOCK), jnp.float32),
        ),
        in_specs=[anywhere] * 5,
        out_specs=(vmem,) * 3,
        scratch_shapes=[
            pltpu.SMEM((4,), jnp.int32),
            pltpu.SMEM((POS_BUCKETS,), jnp.float32),
            pltpu.SMEM((TIME_BUCKETS,), jnp.float32),
            pltpu.VMEM((ROWS // TILE, TILE), jnp.int32),
            pltpu.VMEM((ROWS // TILE, TILE, TILE), jnp.float32),
            pltpu.SemaphoreType.DMA((5,)),
        ],
        compiler_params=pltpu.CompilerParams(vmem_limit_bytes=VMEM_PREPARE * 2**20),
        cost_estimate=pl.CostEstimate(flops=2 * 10**7, bytes_accessed=5 * 10**6, transcendentals=0),
    )(lengths, pos_table, time_table, tokens, stamps)


def half_silu(z):
    return z + z * jnp.tanh(z)


def main_kernel(
    tokens, normed, bias, *refs
):
    planes_hbm, updated_hbm = refs[:8], refs[8]
    planes, in_weight, out_weight, mixed, totals, updated, sems, out_sems = refs[9:]
    dp, own_x = lax.axis_index("dp"), lax.axis_index("group")
    own_m, own_odd = dp // 16, lax.rem(dp // 8, 2)
    own_y, own_core = lax.rem(dp // 2, 4), lax.rem(dp, 2)
    def fetch(k, source, target):
        copy = pltpu.make_async_copy(source, target, sems.at[k])
        copy.start()
        return copy

    copies_in = []
    for side in range(2):
        core = own_core if side == 0 else 1 - own_core
        place = jnp.where(core == 0, own_y, own_x)
        for k in range(4):
            copies_in.append(
                fetch(
                    side * 4 + k,
                    planes_hbm[side * 4 + k],
                    planes.at[core * 4 + lax.rem(place + 4 - k, 4)],
                )
            )

    for copy in copies_in:
        copy.wait()

    def arrange(at, carry):
        m, y = at // 4, lax.rem(at, 4)
        m_slot = lax.rem(own_m + 4 - m, 4)
        units = []
        for core in range(2):
            for x in range(4):
                if core == 0:
                    plane, slot = y, lax.rem(own_x + 4 - x, 4)
                else:
                    plane, slot = 4 + x, lax.rem(own_y + 4 - y, 4)
                start = pl.multiple_of((slot * 4 + m_slot) * 16, 16)
                units.append(planes[plane, pl.ds(start, 16), :].astype(jnp.float32))
        for half in range(2):
            odd = own_odd if half == 0 else 1 - own_odd
            halves = [unit[half * 8 : half * 8 + 8] for unit in units]
            start = pl.multiple_of(m * 512 + odd * 256 + y * 64, 64)
            in_weight[pl.ds(start, 64), :] = jnp.concatenate(
                [piece[:, :D] for piece in halves]
            ).astype(jnp.bfloat16)
            sides = [
                jnp.concatenate([piece[:, D:] for piece in halves[c * 4 : c * 4 + 4]], axis=1)
                for c in range(2)
            ]
            start = pl.multiple_of(m * 128 + odd * 64 + y * 16, 16)
            out_weight[pl.ds(start, 16), :] = jnp.concatenate(sides).astype(jnp.bfloat16)
        return carry

    lax.fori_loop(0, 16, arrange, 0)
    sends = []
    for i in range(ROWS // BLOCK):
        rows = pl.ds(i * BLOCK, BLOCK)
        for part in range(4):
            cols = pl.ds(part * D, D)
            product = lax.dot_general(
                normed[rows, :], in_weight[cols, :], TRANS_B, preferred_element_type=jnp.float32
            )
            mixed[rows, cols] = half_silu(product * 0.5).astype(jnp.bfloat16)

        def attend(j, first, i=i, rows=rows):
            keys = pl.ds(j * BLOCK, BLOCK)
            pair_bias = bias[PAIRS.index((i, j))]
            for head in range(HEADS):
                cols = [pl.ds(part * D + head * HEAD_DIM, HEAD_DIM) for part in range(4)]
                scores = lax.dot_general(
                    mixed[rows, cols[2]], mixed[keys, cols[3]], TRANS_B,
                    preferred_element_type=jnp.float32,
                )
                weights = half_silu(scores * (0.5 * HEAD_DIM**-0.5) + pair_bias).astype(jnp.bfloat16)
                product = jnp.dot(weights, mixed[keys, cols[1]], preferred_element_type=jnp.float32)
                own = pl.ds(head * HEAD_DIM, HEAD_DIM)
                totals[:, own] = product if first else totals[:, own] + product

        attend(i, True)
        for j in range(i):
            attend(j, False)
        attended = totals[...].astype(jnp.bfloat16).astype(jnp.float32)
        gate = mixed[rows, pl.ds(0, D)].astype(jnp.float32)
        gated = (normalize(attended) * gate).astype(jnp.bfloat16)
        projected = lax.dot_general(
            gated, out_weight[...], TRANS_B, preferred_element_type=jnp.float32
        )
        updated[rows, :] = (tokens[rows, :].astype(jnp.float32) + projected).astype(jnp.bfloat16)
        copy = pltpu.make_async_copy(updated.at[rows, :], updated_hbm.at[rows, :], out_sems.at[i])
        copy.start()
        sends.append(copy)
    for copy in sends:
        copy.wait()


def main(tokens, normed, bias, planes):
    anywhere = pl.BlockSpec(memory_space=pl.ANY)
    vmem = pl.BlockSpec(memory_space=pltpu.VMEM)
    return pl.pallas_call(
        main_kernel,
        out_shape=jax.ShapeDtypeStruct((ROWS, D), jnp.bfloat16),
        in_specs=[vmem] * 3 + [anywhere] * 8,
        out_specs=anywhere,
        scratch_shapes=[
            pltpu.VMEM((8, 256, 640), jnp.bfloat16),
            pltpu.VMEM((4 * D, D), jnp.bfloat16),
            pltpu.VMEM((D, D), jnp.bfloat16),
            pltpu.VMEM((ROWS, 4 * D), jnp.bfloat16),
            pltpu.VMEM((BLOCK, D), jnp.float32),
            pltpu.VMEM((ROWS, D), jnp.bfloat16),
            pltpu.SemaphoreType.DMA((8,)),
            pltpu.SemaphoreType.DMA((ROWS // BLOCK,)),
        ],
        compiler_params=pltpu.CompilerParams(vmem_limit_bytes=VMEM_MAIN * 2**20),
        cost_estimate=pl.CostEstimate(
            flops=5 * 10**9, bytes_accessed=9 * 10**6, transcendentals=4 * 10**6
        ),
    )(tokens, normed, bias, *planes)


def device_of(x, y, z, core):
    return ((z % 8 * 4 + y % 4) * 2 + core % 2) * 4 + x % 4


def moves(step):
    return [
        (device_of(x, y, z, core), device_of(*step(x, y, z, core)))
        for z in range(8)
        for y in range(4)
        for core in range(2)
        for x in range(4)
    ]


def send(array, step):
    return lax.ppermute(array, ("dp", "group"), moves(step))


def gather(in_weight, out_weight):
    group = lax.axis_index("group")
    own = lax.dynamic_slice_in_dim(out_weight.T, group * HEAD_DIM, HEAD_DIM, axis=1)
    piece = jnp.concatenate([in_weight.T, own], axis=1)
    other = send(piece, lambda x, y, z, core: (x, y, z ^ 1, core))
    unit = jnp.concatenate([piece, other])
    units = [unit] + [
        send(unit, lambda x, y, z, core, k=k: (x, y, z + 2 * k, core)) for k in (1, 2, 3)
    ]
    line = jnp.concatenate(units)
    lines = [line] + [
        send(line, lambda x, y, z, core, k=k: (x + k * (1 - core), y + k * core, z, core))
        for k in (1, 2, 3)
    ]
    plane = jnp.concatenate(lines)
    return [plane] + [
        send(plane, lambda x, y, z, core, k=k: (x + k * core, y + k * (1 - core), z, core))
        for k in (1, 2, 3)
    ]


def swap(planes):
    return [send(plane, lambda x, y, z, core: (x, y, z, core + 1)) for plane in planes]


def shards(tokens, stamps, lengths, in_weight, out_weight, pos_table, time_table):
    own_lengths = lengths.reshape(-1)
    prepared = prepare(own_lengths, pos_table, time_table, tokens, stamps.reshape(8, TILE))
    own, *others = gather(in_weight, out_weight)
    others, prepared = lax.optimization_barrier((others, prepared))
    planes = [own, *others]
    return main(*prepared, planes + swap(planes))


def solution(mesh):
    return jax.shard_map(
        shards,
        mesh=mesh,
        in_specs=(
            P(("dp", "group"), None),
            P(("dp", "group")),
            P("dp", "group", None),
            P(None, ("dp", "group")),
            P(None, "dp"),
            P(),
            P(),
        ),
        out_specs=P(("dp", "group"), None),
        check_vma=False,
    )
```

```python
import jax
import jax.numpy as jnp
from jax import lax
from jax.experimental import pallas as pl
from jax.experimental.pallas import tpu as pltpu
from jax.sharding import PartitionSpec as P

D = 512
HEADS = 4
HEAD_DIM = 128
ROWS = 1024
BLOCK = 256
TILE = 128
POS_BUCKETS = 12
TIME_BUCKETS = 20
NEVER = -1e30
VMEM_PREPARE = 16
VMEM_MAIN = 32
TRANS_B = (((1,), (1,)), ((), ()))
PAIRS = [(i, j) for i in range(ROWS // BLOCK) for j in range(i + 1)]


def normalize(values):
    center = values - jnp.mean(values, axis=-1, keepdims=True)
    spread = jnp.mean(center * center, axis=-1, keepdims=True)
    return center * lax.rsqrt(spread + 1e-05)


def prepare_kernel(
    lengths_hbm, pos_hbm, time_hbm, tokens_hbm, stamps_hbm, tokens, normed, bias,
    lengths, pos_table, time_table, stamps, pos_tiles, sems,
):
    copies = [
        pltpu.make_async_copy(source, target, sems.at[k])
        for k, (source, target) in enumerate(
            [
                (lengths_hbm, lengths),
                (pos_hbm, pos_table),
                (time_hbm, time_table),
                (stamps_hbm, stamps),
                (tokens_hbm, tokens),
            ]
        )
    ]
    for copy in copies:
        copy.start()
    for copy in copies:
        copy.wait()
    for i in range(ROWS // BLOCK):
        rows = slice(i * BLOCK, (i + 1) * BLOCK)
        normed[rows, :] = normalize(tokens[rows, :].astype(jnp.float32)).astype(jnp.bfloat16)

    apart = lax.broadcasted_iota(jnp.int32, (TILE, TILE), 0) - lax.broadcasted_iota(
        jnp.int32, (TILE, TILE), 1
    )
    for d in range(ROWS // TILE):
        offset = apart + d * TILE
        tile = jnp.full((TILE, TILE), pos_table[0] * 0.5, jnp.float32)
        for power in range(1, POS_BUCKETS):
            if 2**power - 1 <= (d + 1) * TILE - 1:
                tile = jnp.where(offset + 1 >= 2**power, pos_table[power] * 0.5, tile)
        pos_tiles[d] = jnp.where(offset >= 0, tile, NEVER)

    first = lengths[0]
    second = first + lengths[1]
    third = second + lengths[2]
    row_id = (
        lax.broadcasted_iota(jnp.int32, (8, TILE), 0) * TILE
        + lax.broadcasted_iota(jnp.int32, (8, TILE), 1)
    )
    segment = (
        (row_id >= first).astype(jnp.int32)
        + (row_id >= second).astype(jnp.int32)
        + (row_id >= third).astype(jnp.int32)
    )
    times = stamps[...] + segment * (1 << 20)

    lane = lax.broadcasted_iota(jnp.int32, (TILE, TILE), 1)
    lookup = jnp.full((TILE, TILE), NEVER, jnp.float32)
    for entry in range(TIME_BUCKETS):
        lookup = jnp.where(lane == 31 - entry, time_table[entry] * 0.5, lookup)

    for i in range(ROWS // TILE):
        own = jnp.transpose(jnp.broadcast_to(times[i : i + 1, :], (TILE, TILE)))
        own = own + 1
        for j in range(ROWS // TILE):
            qi, kj = i // 2, j // 2
            if kj > qi:
                continue
            at = PAIRS.index((qi, kj))
            rows, cols = pl.ds((i % 2) * TILE, TILE), pl.ds((j % 2) * TILE, TILE)
            if j > i:
                bias[at, rows, cols] = jnp.full((TILE, TILE), NEVER, jnp.float32)
                continue
            gap = own - times[j : j + 1, :]
            time_bias = jnp.take_along_axis(lookup, lax.clz(gap), axis=1)
            bias[at, rows, cols] = time_bias + pos_tiles[i - j]


def prepare(lengths, pos_table, time_table, tokens, stamps):
    hbm = pl.BlockSpec(memory_space=pltpu.HBM)
    vmem = pl.BlockSpec(memory_space=pltpu.VMEM)
    return pl.pallas_call(
        prepare_kernel,
        out_shape=(
            jax.ShapeDtypeStruct((ROWS, D), jnp.bfloat16),
            jax.ShapeDtypeStruct((ROWS, D), jnp.bfloat16),
            jax.ShapeDtypeStruct((len(PAIRS), BLOCK, BLOCK), jnp.float32),
        ),
        in_specs=[hbm] * 5,
        out_specs=(vmem,) * 3,
        scratch_shapes=[
            pltpu.SMEM((4,), jnp.int32),
            pltpu.SMEM((POS_BUCKETS,), jnp.float32),
            pltpu.SMEM((TIME_BUCKETS,), jnp.float32),
            pltpu.VMEM((ROWS // TILE, TILE), jnp.int32),
            pltpu.VMEM((ROWS // TILE, TILE, TILE), jnp.float32),
            pltpu.SemaphoreType.DMA((5,)),
        ],
        compiler_params=pltpu.CompilerParams(vmem_limit_bytes=VMEM_PREPARE * 2**20),
        cost_estimate=pl.CostEstimate(flops=2 * 10**7, bytes_accessed=5 * 10**6, transcendentals=0),
    )(
        *[
            pltpu.with_memory_space_constraint(array, pltpu.HBM)
            for array in (lengths, pos_table, time_table, tokens, stamps)
        ]
    )


def half_silu(z):
    return z + z * jnp.tanh(z)


def main_kernel(
    tokens, normed, bias, *refs
):
    planes_hbm, updated_hbm = refs[:8], refs[8]
    planes, in_weight, out_weight, mixed, totals, updated, sems, out_sems = refs[9:]
    dp, own_x = lax.axis_index("dp"), lax.axis_index("group")
    own_z = dp // 8
    own_odd = lax.rem(own_z, 2)
    own_y, own_core = lax.rem(dp // 2, 4), lax.rem(dp, 2)
    def fetch(k, source, target):
        copy = pltpu.make_async_copy(source, target, sems.at[k])
        copy.start()
        return copy

    copies_in = []
    for side in range(2):
        core = own_core if side == 0 else 1 - own_core
        place = jnp.where(core == 0, own_y, own_x)
        for k in range(4):
            copies_in.append(
                fetch(
                    side * 4 + k,
                    planes_hbm[side * 4 + k],
                    planes.at[core * 4 + lax.rem(place + 4 - k, 4)],
                )
            )

    for copy in copies_in:
        copy.wait()

    def arrange(y, carry):
        for slot in range(8):
            z = lax.rem(own_z - own_odd + 8 - slot // 2 * 2, 8) + jnp.where(slot % 2 == 0, own_odd, 1 - own_odd)
            pieces = []
            for core in range(2):
                for x in range(4):
                    if core == 0:
                        plane, line = y, lax.rem(own_x + 4 - x, 4)
                    else:
                        plane, line = 4 + x, lax.rem(own_y + 4 - y, 4)
                    pieces.append(planes[plane, line * 8 + slot].astype(jnp.float32))
            start = pl.multiple_of(z * 256 + y * 64, 64)
            in_weight[pl.ds(start, 64), :] = jnp.concatenate(
                [piece[:, :D] for piece in pieces]
            ).astype(jnp.bfloat16)
            start = pl.multiple_of(z * 64 + y * 16, 16)
            out_weight[pl.ds(start, 16), :] = jnp.concatenate(
                [
                    jnp.concatenate([piece[:, D:] for piece in pieces[c * 4 : c * 4 + 4]], axis=1)
                    for c in range(2)
                ]
            ).astype(jnp.bfloat16)
        return carry

    lax.fori_loop(0, 4, arrange, 0)
    for i in range(ROWS // 256):
        rows = pl.ds(i * 256, 256)
        for part in range(4):
            cols = pl.ds(part * 512, 512)
            product = lax.dot_general(
                normed[rows, :], in_weight[cols, :], TRANS_B, preferred_element_type=jnp.float32
            )
            mixed[rows, cols] = half_silu(product * 0.5).astype(jnp.bfloat16)
    def finish(i):
        rows = pl.ds(i * BLOCK, BLOCK)
        attended = totals[rows, :].astype(jnp.bfloat16).astype(jnp.float32)
        gate = mixed[rows, pl.ds(0, D)].astype(jnp.float32)
        gated = (normalize(attended) * gate).astype(jnp.bfloat16)
        projected = lax.dot_general(
            gated, out_weight[...], TRANS_B, preferred_element_type=jnp.float32
        )
        updated[rows, :] = (tokens[rows, :].astype(jnp.float32) + projected).astype(jnp.bfloat16)
        copy = pltpu.make_async_copy(updated.at[rows, :], updated_hbm.at[rows, :], out_sems.at[i])
        copy.start()
        sends.append(copy)

    sends = []
    for j in range(ROWS // BLOCK):
        rows = pl.ds(j * BLOCK, ROWS - j * BLOCK)
        keys = pl.ds(j * BLOCK, BLOCK)
        pair_bias = jnp.concatenate([bias[PAIRS.index((i, j))] for i in range(j, ROWS // BLOCK)])
        for head in range(HEADS):
            cols = [pl.ds(part * D + head * HEAD_DIM, HEAD_DIM) for part in range(4)]
            scores = lax.dot_general(
                mixed[rows, cols[2]], mixed[keys, cols[3]], TRANS_B,
                preferred_element_type=jnp.float32,
            )
            weights = half_silu(scores * (0.5 * HEAD_DIM**-0.5) + pair_bias).astype(jnp.bfloat16)
            product = jnp.dot(weights, mixed[keys, cols[1]], preferred_element_type=jnp.float32)
            own = pl.ds(head * HEAD_DIM, HEAD_DIM)
            totals[rows, own] = product if j == 0 else totals[rows, own] + product
    for i in range(ROWS // BLOCK):
        finish(i)
    for copy in sends:
        copy.wait()


def main(tokens, normed, bias, planes):
    anywhere = pl.BlockSpec(memory_space=pl.ANY)
    vmem = pl.BlockSpec(memory_space=pltpu.VMEM)
    return pl.pallas_call(
        main_kernel,
        out_shape=jax.ShapeDtypeStruct((ROWS, D), jnp.bfloat16),
        in_specs=[vmem] * 3 + [anywhere] * 8,
        out_specs=anywhere,
        scratch_shapes=[
            pltpu.VMEM((8, 32, 8, D + HEAD_DIM), jnp.bfloat16),
            pltpu.VMEM((4 * D, D), jnp.bfloat16),
            pltpu.VMEM((D, D), jnp.bfloat16),
            pltpu.VMEM((ROWS, 4 * D), jnp.bfloat16),
            pltpu.VMEM((ROWS, D), jnp.float32),
            pltpu.VMEM((ROWS, D), jnp.bfloat16),
            pltpu.SemaphoreType.DMA((8,)),
            pltpu.SemaphoreType.DMA((ROWS // BLOCK,)),
        ],
        compiler_params=pltpu.CompilerParams(vmem_limit_bytes=VMEM_MAIN * 2**20),
        cost_estimate=pl.CostEstimate(
            flops=5 * 10**9, bytes_accessed=9 * 10**6, transcendentals=4 * 10**6
        ),
    )(tokens, normed, bias, *planes)


def device_of(x, y, z, core):
    return ((z % 8 * 4 + y % 4) * 2 + core % 2) * 4 + x % 4


def moves(step):
    return [
        (device_of(x, y, z, core), device_of(*step(x, y, z, core)))
        for z in range(8)
        for y in range(4)
        for core in range(2)
        for x in range(4)
    ]


def send(array, step):
    return lax.ppermute(array, ("dp", "group"), moves(step))


def gather(in_weight, out_weight):
    group = lax.axis_index("group")
    own = lax.dynamic_slice_in_dim(out_weight.T, group * HEAD_DIM, HEAD_DIM, axis=1)
    piece = jnp.concatenate([in_weight.T, own], axis=1)[None]
    other = send(piece, lambda x, y, z, core: (x, y, z ^ 1, core))
    unit = jnp.concatenate([piece, other])
    units = [unit] + [
        send(unit, lambda x, y, z, core, k=k: (x, y, z + 2 * k, core)) for k in (1, 2, 3)
    ]
    line = jnp.concatenate(units)
    lines = [line] + [
        send(line, lambda x, y, z, core, k=k: (x + k * (1 - core), y + k * core, z, core))
        for k in (1, 2, 3)
    ]
    plane = jnp.concatenate(lines)
    return [plane] + [
        send(plane, lambda x, y, z, core, k=k: (x + k * core, y + k * (1 - core), z, core))
        for k in (1, 2, 3)
    ]


def swap(planes):
    return [send(plane, lambda x, y, z, core: (x, y, z, core + 1)) for plane in planes]


def shards(tokens, stamps, lengths, in_weight, out_weight, pos_table, time_table):
    own_lengths = lengths.reshape(-1)
    planes = gather(in_weight, out_weight)
    swapped = swap(planes[:1])
    swapped, stamps = lax.optimization_barrier((swapped, stamps))
    prepared = prepare(own_lengths, pos_table, time_table, tokens, stamps.reshape(8, TILE))
    planes[1], prepared = lax.optimization_barrier((planes[1], prepared))
    swapped += swap(planes[1:2])
    return main(*prepared, planes + swapped + swap(planes[2:]))


def solution(mesh):
    return jax.shard_map(
        shards,
        mesh=mesh,
        in_specs=(
            P(("dp", "group"), None),
            P(("dp", "group")),
            P("dp", "group", None),
            P(None, ("dp", "group")),
            P(None, "dp"),
            P(),
            P(),
        ),
        out_specs=P(("dp", "group"), None),
        check_vma=False,
    )
```

```python
import jax
import jax.numpy as jnp
from jax import lax
from jax.experimental import pallas as pl
from jax.experimental.pallas import tpu as pltpu
from jax.sharding import PartitionSpec as P

D = 512
HEADS = 4
HEAD_DIM = 128
ROWS = 1024
BLOCK = 256
TILE = 128
POS_BUCKETS = 12
TIME_BUCKETS = 20
NEVER = -1e30
STEPS = (0, -1, 1, 2, -2, -3, 3, 4)
VMEM_PREPARE = 16
VMEM_MAIN = 32
TRANS_B = (((1,), (1,)), ((), ()))
PAIRS = [(i, j) for i in range(ROWS // BLOCK) for j in range(i + 1)]


def normalize(values):
    center = values - jnp.mean(values, axis=-1, keepdims=True)
    spread = jnp.mean(center * center, axis=-1, keepdims=True)
    return center * lax.rsqrt(spread + 1e-05)


def prepare_kernel(
    lengths_hbm, pos_hbm, time_hbm, tokens_hbm, stamps_hbm, tokens, normed, bias,
    lengths, pos_table, time_table, stamps, pos_tiles, sems,
):
    copies = [
        pltpu.make_async_copy(source, target, sems.at[k])
        for k, (source, target) in enumerate(
            [
                (lengths_hbm, lengths),
                (pos_hbm, pos_table),
                (time_hbm, time_table),
                (stamps_hbm, stamps),
                (tokens_hbm, tokens),
            ]
        )
    ]
    for copy in copies:
        copy.start()
    for copy in copies:
        copy.wait()
    for i in range(ROWS // BLOCK):
        rows = slice(i * BLOCK, (i + 1) * BLOCK)
        normed[rows, :] = normalize(tokens[rows, :].astype(jnp.float32)).astype(jnp.bfloat16)

    apart = lax.broadcasted_iota(jnp.int32, (TILE, TILE), 0) - lax.broadcasted_iota(
        jnp.int32, (TILE, TILE), 1
    )
    for d in range(ROWS // TILE):
        offset = apart + d * TILE
        tile = jnp.full((TILE, TILE), pos_table[0] * 0.5, jnp.float32)
        for power in range(1, POS_BUCKETS):
            if 2**power - 1 <= (d + 1) * TILE - 1:
                tile = jnp.where(offset + 1 >= 2**power, pos_table[power] * 0.5, tile)
        pos_tiles[d] = jnp.where(offset >= 0, tile, NEVER)

    first = lengths[0]
    second = first + lengths[1]
    third = second + lengths[2]
    row_id = (
        lax.broadcasted_iota(jnp.int32, (8, TILE), 0) * TILE
        + lax.broadcasted_iota(jnp.int32, (8, TILE), 1)
    )
    segment = (
        (row_id >= first).astype(jnp.int32)
        + (row_id >= second).astype(jnp.int32)
        + (row_id >= third).astype(jnp.int32)
    )
    times = stamps[...] + segment * (1 << 20)

    lane = lax.broadcasted_iota(jnp.int32, (TILE, TILE), 1)
    lookup = jnp.full((TILE, TILE), NEVER, jnp.float32)
    for entry in range(TIME_BUCKETS):
        lookup = jnp.where(lane == 31 - entry, time_table[entry] * 0.5, lookup)

    for i in range(ROWS // TILE):
        own = jnp.transpose(jnp.broadcast_to(times[i : i + 1, :], (TILE, TILE)))
        own = own + 1
        for j in range(ROWS // TILE):
            qi, kj = i // 2, j // 2
            if kj > qi:
                continue
            at = PAIRS.index((qi, kj))
            rows, cols = pl.ds((i % 2) * TILE, TILE), pl.ds((j % 2) * TILE, TILE)
            if j > i:
                bias[at, rows, cols] = jnp.full((TILE, TILE), NEVER, jnp.float32)
                continue
            gap = own - times[j : j + 1, :]
            time_bias = jnp.take_along_axis(lookup, lax.clz(gap), axis=1)
            bias[at, rows, cols] = time_bias + pos_tiles[i - j]


def prepare(lengths, pos_table, time_table, tokens, stamps):
    hbm = pl.BlockSpec(memory_space=pltpu.HBM)
    vmem = pl.BlockSpec(memory_space=pltpu.VMEM)
    return pl.pallas_call(
        prepare_kernel,
        out_shape=(
            jax.ShapeDtypeStruct((ROWS, D), jnp.bfloat16),
            jax.ShapeDtypeStruct((ROWS, D), jnp.bfloat16),
            jax.ShapeDtypeStruct((len(PAIRS), BLOCK, BLOCK), jnp.float32),
        ),
        in_specs=[hbm] * 5,
        out_specs=(vmem,) * 3,
        scratch_shapes=[
            pltpu.SMEM((4,), jnp.int32),
            pltpu.SMEM((POS_BUCKETS,), jnp.float32),
            pltpu.SMEM((TIME_BUCKETS,), jnp.float32),
            pltpu.VMEM((ROWS // TILE, TILE), jnp.int32),
            pltpu.VMEM((ROWS // TILE, TILE, TILE), jnp.float32),
            pltpu.SemaphoreType.DMA((5,)),
        ],
        compiler_params=pltpu.CompilerParams(vmem_limit_bytes=VMEM_PREPARE * 2**20),
        cost_estimate=pl.CostEstimate(flops=2 * 10**7, bytes_accessed=5 * 10**6, transcendentals=0),
    )(
        *[
            pltpu.with_memory_space_constraint(array, pltpu.HBM)
            for array in (lengths, pos_table, time_table, tokens, stamps)
        ]
    )


def half_silu(z):
    return z + z * jnp.tanh(z)


def line_slot(apart):
    apart = lax.rem(apart, 4)
    slot = jnp.where(apart == 1, 1, jnp.where(apart == 2, 3, 2))
    return jnp.where(apart == 0, 0, slot)


def main_kernel(
    tokens, normed, bias, *refs
):
    planes_hbm, updated_hbm = refs[:8], refs[8]
    planes, in_weight, out_weight, mixed, totals, updated, sems, out_sems = refs[9:]
    dp, own_x = lax.axis_index("dp"), lax.axis_index("group")
    own_z = dp // 8
    own_odd = lax.rem(own_z, 2)
    own_y, own_core = lax.rem(dp // 2, 4), lax.rem(dp, 2)
    def fetch(k, source, target):
        copy = pltpu.make_async_copy(source, target, sems.at[k])
        copy.start()
        return copy

    copies_in = []
    for side in range(2):
        core = own_core if side == 0 else 1 - own_core
        place = jnp.where(core == 0, own_y, own_x)
        for k in range(4):
            copies_in.append(
                fetch(
                    side * 4 + k,
                    planes_hbm[side * 4 + k],
                    planes.at[core * 4 + lax.rem(place + 4 - k, 4)],
                )
            )

    for copy in copies_in:
        copy.wait()

    def arrange(y, carry):
        for slot in range(8):
            z = lax.rem(own_z + 8 + jnp.where(own_odd == 1, STEPS[slot], -STEPS[slot]), 8)
            pieces = []
            for core in range(2):
                for x in range(4):
                    if core == 0:
                        plane, line = y, line_slot(own_x + 4 - x)
                    else:
                        plane, line = 4 + x, line_slot(own_y + 4 - y)
                    pieces.append(planes[plane, line * 8 + slot].astype(jnp.float32))
            start = pl.multiple_of(z * 256 + y * 64, 64)
            in_weight[pl.ds(start, 64), :] = jnp.concatenate(
                [piece[:, :D] for piece in pieces]
            ).astype(jnp.bfloat16)
            start = pl.multiple_of(z * 64 + y * 16, 16)
            out_weight[pl.ds(start, 16), :] = jnp.concatenate(
                [
                    jnp.concatenate([piece[:, D:] for piece in pieces[c * 4 : c * 4 + 4]], axis=1)
                    for c in range(2)
                ]
            ).astype(jnp.bfloat16)
        return carry

    lax.fori_loop(0, 4, arrange, 0)
    for i in range(ROWS // 256):
        rows = pl.ds(i * 256, 256)
        for part in range(4):
            cols = pl.ds(part * 512, 512)
            product = lax.dot_general(
                normed[rows, :], in_weight[cols, :], TRANS_B, preferred_element_type=jnp.float32
            )
            mixed[rows, cols] = half_silu(product * 0.5).astype(jnp.bfloat16)
    def finish(i):
        rows = pl.ds(i * BLOCK, BLOCK)
        attended = totals[rows, :].astype(jnp.bfloat16).astype(jnp.float32)
        gate = mixed[rows, pl.ds(0, D)].astype(jnp.float32)
        gated = (normalize(attended) * gate).astype(jnp.bfloat16)
        projected = lax.dot_general(
            gated, out_weight[...], TRANS_B, preferred_element_type=jnp.float32
        )
        updated[rows, :] = (tokens[rows, :].astype(jnp.float32) + projected).astype(jnp.bfloat16)
        copy = pltpu.make_async_copy(updated.at[rows, :], updated_hbm.at[rows, :], out_sems.at[i])
        copy.start()
        sends.append(copy)

    sends = []
    for j in range(ROWS // BLOCK):
        rows = pl.ds(j * BLOCK, ROWS - j * BLOCK)
        keys = pl.ds(j * BLOCK, BLOCK)
        pair_bias = jnp.concatenate([bias[PAIRS.index((i, j))] for i in range(j, ROWS // BLOCK)])
        for head in range(HEADS):
            cols = [pl.ds(part * D + head * HEAD_DIM, HEAD_DIM) for part in range(4)]
            scores = lax.dot_general(
                mixed[rows, cols[2]], mixed[keys, cols[3]], TRANS_B,
                preferred_element_type=jnp.float32,
            )
            weights = half_silu(scores * (0.5 * HEAD_DIM**-0.5) + pair_bias).astype(jnp.bfloat16)
            product = jnp.dot(weights, mixed[keys, cols[1]], preferred_element_type=jnp.float32)
            own = pl.ds(head * HEAD_DIM, HEAD_DIM)
            totals[rows, own] = product if j == 0 else totals[rows, own] + product
    for i in range(ROWS // BLOCK):
        finish(i)
    for copy in sends:
        copy.wait()


def main(tokens, normed, bias, planes):
    anywhere = pl.BlockSpec(memory_space=pl.ANY)
    vmem = pl.BlockSpec(memory_space=pltpu.VMEM)
    return pl.pallas_call(
        main_kernel,
        out_shape=jax.ShapeDtypeStruct((ROWS, D), jnp.bfloat16),
        in_specs=[vmem] * 3 + [anywhere] * 8,
        out_specs=anywhere,
        scratch_shapes=[
            pltpu.VMEM((8, 32, 8, D + HEAD_DIM), jnp.bfloat16),
            pltpu.VMEM((4 * D, D), jnp.bfloat16),
            pltpu.VMEM((D, D), jnp.bfloat16),
            pltpu.VMEM((ROWS, 4 * D), jnp.bfloat16),
            pltpu.VMEM((ROWS, D), jnp.float32),
            pltpu.VMEM((ROWS, D), jnp.bfloat16),
            pltpu.SemaphoreType.DMA((8,)),
            pltpu.SemaphoreType.DMA((ROWS // BLOCK,)),
        ],
        compiler_params=pltpu.CompilerParams(vmem_limit_bytes=VMEM_MAIN * 2**20),
        cost_estimate=pl.CostEstimate(
            flops=5 * 10**9, bytes_accessed=9 * 10**6, transcendentals=4 * 10**6
        ),
    )(tokens, normed, bias, *planes)


def device_of(x, y, z, core):
    return ((z % 8 * 4 + y % 4) * 2 + core % 2) * 4 + x % 4


def moves(step):
    return [
        (device_of(x, y, z, core), device_of(*step(x, y, z, core)))
        for z in range(8)
        for y in range(4)
        for core in range(2)
        for x in range(4)
    ]


def send(array, step):
    return lax.ppermute(array, ("dp", "group"), moves(step))


def gather(in_weight, out_weight):
    group = lax.axis_index("group")
    own = lax.dynamic_slice_in_dim(out_weight.T, group * HEAD_DIM, HEAD_DIM, axis=1)
    piece = jnp.concatenate([in_weight.T, own], axis=1)[None]
    other = send(piece, lambda x, y, z, core: (x, y, z ^ 1, core))
    unit = jnp.concatenate([piece, other])
    units = [
        unit,
        send(unit, lambda x, y, z, core: (x, y, z + 2 * (z % 2) - 1, core)),
        send(unit, lambda x, y, z, core: (x, y, z + 4 * (z % 2) - 2, core)),
        send(unit, lambda x, y, z, core: (x, y, z + 6 * (z % 2) - 3, core)),
    ]
    line = jnp.concatenate(units)
    lines = [line] + [
        send(line, lambda x, y, z, core, k=k: (x + k * (1 - core), y + k * core, z, core))
        for k in (1, 3, 2)
    ]
    plane = jnp.concatenate(lines)
    return [plane] + [
        send(plane, lambda x, y, z, core, k=k: (x + k * core, y + k * (1 - core), z, core))
        for k in (1, 2, 3)
    ]


def swap(planes):
    return [send(plane, lambda x, y, z, core: (x, y, z, core + 1)) for plane in planes]


def shards(tokens, stamps, lengths, in_weight, out_weight, pos_table, time_table):
    own_lengths = lengths.reshape(-1)
    planes = gather(in_weight, out_weight)
    swapped = swap(planes[:1])
    swapped, stamps = lax.optimization_barrier((swapped, stamps))
    prepared = prepare(own_lengths, pos_table, time_table, tokens, stamps.reshape(8, TILE))
    planes[1], prepared = lax.optimization_barrier((planes[1], prepared))
    swapped += swap(planes[1:2])
    return main(*prepared, planes + swapped + swap(planes[2:]))


def solution(mesh):
    return jax.shard_map(
        shards,
        mesh=mesh,
        in_specs=(
            P(("dp", "group"), None),
            P(("dp", "group")),
            P("dp", "group", None),
            P(None, ("dp", "group")),
            P(None, "dp"),
            P(),
            P(),
        ),
        out_specs=P(("dp", "group"), None),
        check_vma=False,
    )
```

```python
import jax
import jax.numpy as jnp
from jax import lax
from jax.experimental import pallas as pl
from jax.experimental.pallas import tpu as pltpu
from jax.sharding import PartitionSpec as P

D = 512
HEADS = 4
HEAD_DIM = 128
ROWS = 1024
BLOCK = 256
TILE = 128
POS_BUCKETS = 12
TIME_BUCKETS = 20
NEVER = -1e30
STEPS = (0, -1, 1, 2, -2, -3, 3, 4)
VMEM_PREPARE = 16
VMEM_MAIN = 32
TRANS_B = (((1,), (1,)), ((), ()))
PAIRS = [(i, j) for i in range(ROWS // BLOCK) for j in range(i + 1)]


def normalize(values):
    center = values - jnp.mean(values, axis=-1, keepdims=True)
    spread = jnp.mean(center * center, axis=-1, keepdims=True)
    return center * lax.rsqrt(spread + 1e-05)


def prepare_kernel(
    lengths_hbm, pos_hbm, time_hbm, tokens_hbm, stamps_hbm, tokens, normed, bias,
    lengths, pos_table, time_table, stamps, pos_tiles, sems,
):
    copies = [
        pltpu.make_async_copy(source, target, sems.at[k])
        for k, (source, target) in enumerate(
            [
                (lengths_hbm, lengths),
                (pos_hbm, pos_table),
                (time_hbm, time_table),
                (stamps_hbm, stamps),
                (tokens_hbm, tokens),
            ]
        )
    ]
    for copy in copies:
        copy.start()
    for copy in copies:
        copy.wait()
    for i in range(ROWS // BLOCK):
        rows = slice(i * BLOCK, (i + 1) * BLOCK)
        normed[rows, :] = normalize(tokens[rows, :].astype(jnp.float32)).astype(jnp.bfloat16)

    apart = lax.broadcasted_iota(jnp.int32, (TILE, TILE), 0) - lax.broadcasted_iota(
        jnp.int32, (TILE, TILE), 1
    )
    for d in range(ROWS // TILE):
        offset = apart + d * TILE
        tile = jnp.full((TILE, TILE), pos_table[0] * 0.5, jnp.float32)
        for power in range(1, POS_BUCKETS):
            if 2**power - 1 <= (d + 1) * TILE - 1:
                tile = jnp.where(offset + 1 >= 2**power, pos_table[power] * 0.5, tile)
        pos_tiles[d] = jnp.where(offset >= 0, tile, NEVER)

    first = lengths[0]
    second = first + lengths[1]
    third = second + lengths[2]
    row_id = (
        lax.broadcasted_iota(jnp.int32, (8, TILE), 0) * TILE
        + lax.broadcasted_iota(jnp.int32, (8, TILE), 1)
    )
    segment = (
        (row_id >= first).astype(jnp.int32)
        + (row_id >= second).astype(jnp.int32)
        + (row_id >= third).astype(jnp.int32)
    )
    times = stamps[...] + segment * (1 << 20)

    lane = lax.broadcasted_iota(jnp.int32, (TILE, TILE), 1)
    lookup = jnp.full((TILE, TILE), NEVER, jnp.float32)
    for entry in range(TIME_BUCKETS):
        lookup = jnp.where(lane == 31 - entry, time_table[entry] * 0.5, lookup)

    for i in range(ROWS // TILE):
        own = jnp.transpose(jnp.broadcast_to(times[i : i + 1, :], (TILE, TILE)))
        own = own + 1
        for j in range(ROWS // TILE):
            qi, kj = i // 2, j // 2
            if kj > qi:
                continue
            at = PAIRS.index((qi, kj))
            rows, cols = pl.ds((i % 2) * TILE, TILE), pl.ds((j % 2) * TILE, TILE)
            if j > i:
                bias[at, rows, cols] = jnp.full((TILE, TILE), NEVER, jnp.float32)
                continue
            gap = own - times[j : j + 1, :]
            time_bias = jnp.take_along_axis(lookup, lax.clz(gap), axis=1)
            bias[at, rows, cols] = time_bias + pos_tiles[i - j]


def prepare(lengths, pos_table, time_table, tokens, stamps):
    hbm = pl.BlockSpec(memory_space=pltpu.HBM)
    vmem = pl.BlockSpec(memory_space=pltpu.VMEM)
    return pl.pallas_call(
        prepare_kernel,
        out_shape=(
            jax.ShapeDtypeStruct((ROWS, D), jnp.bfloat16),
            jax.ShapeDtypeStruct((ROWS, D), jnp.bfloat16),
            jax.ShapeDtypeStruct((len(PAIRS), BLOCK, BLOCK), jnp.float32),
        ),
        in_specs=[hbm] * 5,
        out_specs=(vmem,) * 3,
        scratch_shapes=[
            pltpu.SMEM((4,), jnp.int32),
            pltpu.SMEM((POS_BUCKETS,), jnp.float32),
            pltpu.SMEM((TIME_BUCKETS,), jnp.float32),
            pltpu.VMEM((ROWS // TILE, TILE), jnp.int32),
            pltpu.VMEM((ROWS // TILE, TILE, TILE), jnp.float32),
            pltpu.SemaphoreType.DMA((5,)),
        ],
        compiler_params=pltpu.CompilerParams(vmem_limit_bytes=VMEM_PREPARE * 2**20),
        cost_estimate=pl.CostEstimate(flops=2 * 10**7, bytes_accessed=5 * 10**6, transcendentals=0),
    )(
        *[
            pltpu.with_memory_space_constraint(array, pltpu.HBM)
            for array in (lengths, pos_table, time_table, tokens, stamps)
        ]
    )


def half_silu(z):
    return z + z * jnp.tanh(z)


def line_slot(apart):
    apart = lax.rem(apart, 4)
    slot = jnp.where(apart == 1, 1, jnp.where(apart == 2, 3, 2))
    return jnp.where(apart == 0, 0, slot)


def main_kernel(
    tokens, normed, bias, *refs
):
    own_planes, (swapped_own, swapped_near, swapped_far), updated_hbm = refs[:4], refs[4:7], refs[7]
    planes, in_weight, out_weight, mixed, totals, updated, sems, out_sems = refs[8:]
    near, last = swapped_near.at[pl.ds(0, 32)], swapped_near.at[pl.ds(32, 32)]
    sources = [own_planes, (swapped_own, near, swapped_far, last)]
    dp, own_x = lax.axis_index("dp"), lax.axis_index("group")
    own_z = dp // 8
    own_odd = lax.rem(own_z, 2)
    own_y, own_core = lax.rem(dp // 2, 4), lax.rem(dp, 2)

    def fetch(k, source, target):
        copy = pltpu.make_async_copy(source, target, sems.at[k])
        copy.start()
        return copy

    copies_in = []
    for side in range(2):
        core = own_core if side == 0 else 1 - own_core
        place = jnp.where(core == 0, own_y, own_x)
        for k in range(4):
            copies_in.append(
                fetch(
                    side * 4 + k,
                    sources[side][k],
                    planes.at[core * 4 + lax.rem(place + 4 - k, 4)],
                )
            )

    for copy in copies_in:
        copy.wait()

    def arrange(y, carry):
        for slot in range(8):
            z = lax.rem(own_z + 8 + jnp.where(own_odd == 1, STEPS[slot], -STEPS[slot]), 8)
            pieces = []
            for core in range(2):
                for x in range(4):
                    if core == 0:
                        plane, line = y, line_slot(own_x + 4 - x)
                    else:
                        plane, line = 4 + x, line_slot(own_y + 4 - y)
                    pieces.append(planes[plane, line * 8 + slot].astype(jnp.float32))
            start = pl.multiple_of(z * 256 + y * 64, 64)
            in_weight[pl.ds(start, 64), :] = jnp.concatenate(
                [piece[:, :D] for piece in pieces]
            ).astype(jnp.bfloat16)
            start = pl.multiple_of(z * 64 + y * 16, 16)
            out_weight[pl.ds(start, 16), :] = jnp.concatenate(
                [
                    jnp.concatenate([piece[:, D:] for piece in pieces[c * 4 : c * 4 + 4]], axis=1)
                    for c in range(2)
                ]
            ).astype(jnp.bfloat16)
        return carry

    lax.fori_loop(0, 4, arrange, 0)
    for i in range(ROWS // 256):
        rows = pl.ds(i * 256, 256)
        for part in range(4):
            cols = pl.ds(part * 512, 512)
            product = lax.dot_general(
                normed[rows, :], in_weight[cols, :], TRANS_B, preferred_element_type=jnp.float32
            )
            mixed[rows, cols] = half_silu(product * 0.5).astype(jnp.bfloat16)
    def finish(i):
        rows = pl.ds(i * BLOCK, BLOCK)
        attended = totals[rows, :].astype(jnp.bfloat16).astype(jnp.float32)
        gate = mixed[rows, pl.ds(0, D)].astype(jnp.float32)
        gated = (normalize(attended) * gate).astype(jnp.bfloat16)
        projected = lax.dot_general(
            gated, out_weight[...], TRANS_B, preferred_element_type=jnp.float32
        )
        updated[rows, :] = (tokens[rows, :].astype(jnp.float32) + projected).astype(jnp.bfloat16)
        copy = pltpu.make_async_copy(updated.at[rows, :], updated_hbm.at[rows, :], out_sems.at[i])
        copy.start()
        sends.append(copy)

    sends = []
    for j in range(ROWS // BLOCK):
        rows = pl.ds(j * BLOCK, ROWS - j * BLOCK)
        keys = pl.ds(j * BLOCK, BLOCK)
        pair_bias = jnp.concatenate([bias[PAIRS.index((i, j))] for i in range(j, ROWS // BLOCK)])
        for head in range(HEADS):
            cols = [pl.ds(part * D + head * HEAD_DIM, HEAD_DIM) for part in range(4)]
            scores = lax.dot_general(
                mixed[rows, cols[2]], mixed[keys, cols[3]], TRANS_B,
                preferred_element_type=jnp.float32,
            )
            weights = half_silu(scores * (0.5 * HEAD_DIM**-0.5) + pair_bias).astype(jnp.bfloat16)
            product = jnp.dot(weights, mixed[keys, cols[1]], preferred_element_type=jnp.float32)
            own = pl.ds(head * HEAD_DIM, HEAD_DIM)
            totals[rows, own] = product if j == 0 else totals[rows, own] + product
    for i in range(ROWS // BLOCK):
        finish(i)
    for copy in sends:
        copy.wait()


def main(tokens, normed, bias, planes):
    anywhere = pl.BlockSpec(memory_space=pl.ANY)
    vmem = pl.BlockSpec(memory_space=pltpu.VMEM)
    return pl.pallas_call(
        main_kernel,
        out_shape=jax.ShapeDtypeStruct((ROWS, D), jnp.bfloat16),
        in_specs=[vmem] * 3 + [anywhere] * 7,
        out_specs=anywhere,
        scratch_shapes=[
            pltpu.VMEM((8, 32, 8, D + HEAD_DIM), jnp.bfloat16),
            pltpu.VMEM((4 * D, D), jnp.bfloat16),
            pltpu.VMEM((D, D), jnp.bfloat16),
            pltpu.VMEM((ROWS, 4 * D), jnp.bfloat16),
            pltpu.VMEM((ROWS, D), jnp.float32),
            pltpu.VMEM((ROWS, D), jnp.bfloat16),
            pltpu.SemaphoreType.DMA((8,)),
            pltpu.SemaphoreType.DMA((ROWS // BLOCK,)),
        ],
        compiler_params=pltpu.CompilerParams(vmem_limit_bytes=VMEM_MAIN * 2**20),
        cost_estimate=pl.CostEstimate(
            flops=5 * 10**9, bytes_accessed=9 * 10**6, transcendentals=4 * 10**6
        ),
    )(tokens, normed, bias, *planes)


def device_of(x, y, z, core):
    return ((z % 8 * 4 + y % 4) * 2 + core % 2) * 4 + x % 4


def moves(step):
    return [
        (device_of(x, y, z, core), device_of(*step(x, y, z, core)))
        for z in range(8)
        for y in range(4)
        for core in range(2)
        for x in range(4)
    ]


def send(array, step):
    return lax.ppermute(array, ("dp", "group"), moves(step))


def gather(in_weight, out_weight):
    part = lax.axis_index("group") * HEAD_DIM

    def piece_of(in_rows, out_rows):
        side = lax.dynamic_slice_in_dim(out_rows, part, HEAD_DIM, axis=1)
        return jnp.concatenate([in_rows, side], axis=1)[None]

    piece = piece_of(in_weight.T, out_weight.T)
    other = piece_of(
        send(in_weight.T, lambda x, y, z, core: (x, y, z ^ 1, core)),
        send(out_weight.T, lambda x, y, z, core: (x, y, z ^ 1, core)),
    )
    unit = jnp.concatenate([piece, other])
    units = [
        unit,
        send(unit, lambda x, y, z, core: (x, y, z + 2 * (z % 2) - 1, core)),
        send(unit, lambda x, y, z, core: (x, y, z + 4 * (z % 2) - 2, core)),
        send(unit, lambda x, y, z, core: (x, y, z + 6 * (z % 2) - 3, core)),
    ]
    line = jnp.concatenate(units)
    lines = [line] + [
        send(line, lambda x, y, z, core, k=k: (x + k * (1 - core), y + k * core, z, core))
        for k in (1, 3, 2)
    ]
    plane = jnp.concatenate(lines)
    return [plane] + [
        send(plane, lambda x, y, z, core, k=k: (x + k * core, y + k * (1 - core), z, core))
        for k in (1, 2, 3)
    ]


def swap(array):
    return send(array, lambda x, y, z, core: (x, y, z, core + 1))


def shards(tokens, stamps, lengths, in_weight, out_weight, pos_table, time_table):
    own_lengths = lengths.reshape(-1)
    planes = gather(in_weight, out_weight)
    swapped_own = swap(planes[0])
    swapped_own, stamps = lax.optimization_barrier((swapped_own, stamps))
    prepared = prepare(own_lengths, pos_table, time_table, tokens, stamps.reshape(8, TILE))
    planes[1], prepared = lax.optimization_barrier((planes[1], prepared))
    swapped_near = swap(jnp.concatenate([planes[1], planes[3]]))
    return main(*prepared, [*planes, swapped_own, swapped_near, swap(planes[2])])


def solution(mesh):
    return jax.shard_map(
        shards,
        mesh=mesh,
        in_specs=(
            P(("dp", "group"), None),
            P(("dp", "group")),
            P("dp", "group", None),
            P(None, ("dp", "group")),
            P(None, "dp"),
            P(),
            P(),
        ),
        out_specs=P(("dp", "group"), None),
        check_vma=False,
    )
```

```python
import jax
import jax.numpy as jnp
from jax import lax
from jax.experimental import pallas as pl
from jax.experimental.pallas import tpu as pltpu
from jax.sharding import PartitionSpec as P

D = 512
HEADS = 4
HEAD_DIM = 128
ROWS = 1024
BLOCK = 256
TILE = 128
POS_BUCKETS = 12
TIME_BUCKETS = 20
NEVER = -1e30
STEPS = (0, -1, 1, 2, -2, -3, 3, 4)
VMEM_PREPARE = 16
VMEM_MAIN = 32
TRANS_B = (((1,), (1,)), ((), ()))
PAIRS = [(i, j) for i in range(ROWS // BLOCK) for j in range(i + 1)]


def normalize(values):
    center = values - jnp.mean(values, axis=-1, keepdims=True)
    spread = jnp.mean(center * center, axis=-1, keepdims=True)
    return center * lax.rsqrt(spread + 1e-05)


def prepare_kernel(
    lengths_hbm, pos_hbm, time_hbm, tokens_hbm, stamps_hbm, tokens, normed, bias,
    lengths, pos_table, time_table, stamps, pos_tiles, sems,
):
    copies = [
        pltpu.make_async_copy(source, target, sems.at[k])
        for k, (source, target) in enumerate(
            [
                (lengths_hbm, lengths),
                (pos_hbm, pos_table),
                (time_hbm, time_table),
                (stamps_hbm, stamps),
                (tokens_hbm, tokens),
            ]
        )
    ]
    for copy in copies:
        copy.start()
    for copy in copies:
        copy.wait()
    for i in range(ROWS // BLOCK):
        rows = slice(i * BLOCK, (i + 1) * BLOCK)
        normed[rows, :] = normalize(tokens[rows, :].astype(jnp.float32)).astype(jnp.bfloat16)

    apart = lax.broadcasted_iota(jnp.int32, (TILE, TILE), 0) - lax.broadcasted_iota(
        jnp.int32, (TILE, TILE), 1
    )
    for d in range(ROWS // TILE):
        offset = apart + d * TILE
        tile = jnp.full((TILE, TILE), pos_table[0] * 0.5, jnp.float32)
        for power in range(1, POS_BUCKETS):
            if 2**power - 1 <= (d + 1) * TILE - 1:
                tile = jnp.where(offset + 1 >= 2**power, pos_table[power] * 0.5, tile)
        pos_tiles[d] = jnp.where(offset >= 0, tile, NEVER)

    first = lengths[0]
    second = first + lengths[1]
    third = second + lengths[2]
    row_id = (
        lax.broadcasted_iota(jnp.int32, (8, TILE), 0) * TILE
        + lax.broadcasted_iota(jnp.int32, (8, TILE), 1)
    )
    segment = (
        (row_id >= first).astype(jnp.int32)
        + (row_id >= second).astype(jnp.int32)
        + (row_id >= third).astype(jnp.int32)
    )
    times = stamps[...] + segment * (1 << 20)

    lane = lax.broadcasted_iota(jnp.int32, (TILE, TILE), 1)
    lookup = jnp.full((TILE, TILE), NEVER, jnp.float32)
    for entry in range(TIME_BUCKETS):
        lookup = jnp.where(lane == 31 - entry, time_table[entry] * 0.5, lookup)

    for i in range(ROWS // TILE):
        own = jnp.transpose(jnp.broadcast_to(times[i : i + 1, :], (TILE, TILE)))
        own = own + 1
        for j in range(ROWS // TILE):
            qi, kj = i // 2, j // 2
            if kj > qi:
                continue
            at = PAIRS.index((qi, kj))
            rows, cols = pl.ds((i % 2) * TILE, TILE), pl.ds((j % 2) * TILE, TILE)
            if j > i:
                bias[at, rows, cols] = jnp.full((TILE, TILE), NEVER, jnp.float32)
                continue
            gap = own - times[j : j + 1, :]
            time_bias = jnp.take_along_axis(lookup, lax.clz(gap), axis=1)
            bias[at, rows, cols] = time_bias + pos_tiles[i - j]


def prepare(lengths, pos_table, time_table, tokens, stamps):
    hbm = pl.BlockSpec(memory_space=pltpu.HBM)
    vmem = pl.BlockSpec(memory_space=pltpu.VMEM)
    return pl.pallas_call(
        prepare_kernel,
        out_shape=(
            jax.ShapeDtypeStruct((ROWS, D), jnp.bfloat16),
            jax.ShapeDtypeStruct((ROWS, D), jnp.bfloat16),
            jax.ShapeDtypeStruct((len(PAIRS), BLOCK, BLOCK), jnp.float32),
        ),
        in_specs=[hbm] * 5,
        out_specs=(vmem,) * 3,
        scratch_shapes=[
            pltpu.SMEM((4,), jnp.int32),
            pltpu.SMEM((POS_BUCKETS,), jnp.float32),
            pltpu.SMEM((TIME_BUCKETS,), jnp.float32),
            pltpu.VMEM((ROWS // TILE, TILE), jnp.int32),
            pltpu.VMEM((ROWS // TILE, TILE, TILE), jnp.float32),
            pltpu.SemaphoreType.DMA((5,)),
        ],
        compiler_params=pltpu.CompilerParams(vmem_limit_bytes=VMEM_PREPARE * 2**20),
        cost_estimate=pl.CostEstimate(flops=2 * 10**7, bytes_accessed=5 * 10**6, transcendentals=0),
    )(
        *[
            pltpu.with_memory_space_constraint(array, pltpu.HBM)
            for array in (lengths, pos_table, time_table, tokens, stamps)
        ]
    )


def half_silu(z):
    return z + z * jnp.tanh(z)


def line_slot(apart):
    apart = lax.rem(apart, 4)
    slot = jnp.where(apart == 1, 1, jnp.where(apart == 2, 3, 2))
    return jnp.where(apart == 0, 0, slot)


def coordinates():
    dp = lax.axis_index("dp")
    return lax.axis_index("group"), lax.rem(dp // 2, 4), dp // 8, lax.rem(dp, 2)


def place(source, start, own_core, far, in_weight, out_weight):
    own_x, own_y, own_z, core = coordinates()
    core = core if own_core else 1 - core
    step = jnp.where(lax.rem(own_z, 2) == 1, 1, -1)
    first, second = jnp.where(core == 0, own_x, own_y), jnp.where(core == 0, own_y, own_x)
    second = lax.rem(second + 4 - far, 4)

    def line(apart, carry):
        along = lax.rem(first + 4 - apart, 4)
        x, y = jnp.where(core == 0, along, second), jnp.where(core == 0, second, along)
        lanes = pl.ds(pl.multiple_of(x * HEAD_DIM, HEAD_DIM), HEAD_DIM)
        at = start + line_slot(apart) * 8
        for slot in range(8):
            z = lax.rem(own_z + 8 + step * STEPS[slot], 8)
            piece = source[at + slot]
            in_weight[z * 32 + y * 8 + core * 4 + x] = piece[:, :D]
            out_weight[z * 8 + y * 2 + core, :, lanes] = piece[:, D:]
        return carry

    lax.fori_loop(0, 4, line, 0)


def arrange_kernel(own, near, far, last, swapped_own, swapped_near, in_weight, out_weight):
    for k, source in enumerate((own, near, far, last)):
        place(source, 0, True, k, in_weight, out_weight)
    place(swapped_own, 0, False, 0, in_weight, out_weight)
    place(swapped_near, 0, False, 1, in_weight, out_weight)
    place(swapped_near, 32, False, 3, in_weight, out_weight)


def arrange(planes, swapped_own, swapped_near):
    vmem = pl.BlockSpec(memory_space=pltpu.VMEM)
    return pl.pallas_call(
        arrange_kernel,
        out_shape=(
            jax.ShapeDtypeStruct((4 * D // 8, 8, D), jnp.bfloat16),
            jax.ShapeDtypeStruct((D // 8, 8, D), jnp.bfloat16),
        ),
        in_specs=[vmem] * 6,
        out_specs=(vmem,) * 2,
        compiler_params=pltpu.CompilerParams(vmem_limit_bytes=VMEM_PREPARE * 2**20),
        cost_estimate=pl.CostEstimate(flops=10**6, bytes_accessed=10**6, transcendentals=0),
    )(*planes, swapped_own, swapped_near)


def main_kernel(
    tokens, normed, bias, swapped_far, in_weight_given, out_weight_given,
    updated_hbm, in_weight, out_weight, mixed, totals, updated, out_sems,
):
    place(swapped_far, 0, False, 2, in_weight, out_weight)
    for i in range(ROWS // 256):
        rows = pl.ds(i * 256, 256)
        for part in range(4):
            cols = pl.ds(part * 512, 512)
            product = lax.dot_general(
                normed[rows, :], in_weight[pl.ds(part * (D // 8), D // 8)].reshape(D, D), TRANS_B, preferred_element_type=jnp.float32
            )
            mixed[rows, cols] = half_silu(product * 0.5).astype(jnp.bfloat16)
    def finish(i):
        rows = pl.ds(i * BLOCK, BLOCK)
        attended = totals[rows, :].astype(jnp.bfloat16).astype(jnp.float32)
        gate = mixed[rows, pl.ds(0, D)].astype(jnp.float32)
        gated = (normalize(attended) * gate).astype(jnp.bfloat16)
        projected = lax.dot_general(
            gated, out_weight[...].reshape(D, D), TRANS_B, preferred_element_type=jnp.float32
        )
        updated[rows, :] = (tokens[rows, :].astype(jnp.float32) + projected).astype(jnp.bfloat16)
        copy = pltpu.make_async_copy(updated.at[rows, :], updated_hbm.at[rows, :], out_sems.at[i])
        copy.start()
        sends.append(copy)

    sends = []
    for j in range(ROWS // BLOCK):
        rows = pl.ds(j * BLOCK, ROWS - j * BLOCK)
        keys = pl.ds(j * BLOCK, BLOCK)
        pair_bias = jnp.concatenate([bias[PAIRS.index((i, j))] for i in range(j, ROWS // BLOCK)])
        for head in range(HEADS):
            cols = [pl.ds(part * D + head * HEAD_DIM, HEAD_DIM) for part in range(4)]
            scores = lax.dot_general(
                mixed[rows, cols[2]], mixed[keys, cols[3]], TRANS_B,
                preferred_element_type=jnp.float32,
            )
            weights = half_silu(scores * (0.5 * HEAD_DIM**-0.5) + pair_bias).astype(jnp.bfloat16)
            product = jnp.dot(weights, mixed[keys, cols[1]], preferred_element_type=jnp.float32)
            own = pl.ds(head * HEAD_DIM, HEAD_DIM)
            totals[rows, own] = product if j == 0 else totals[rows, own] + product
    for i in range(ROWS // BLOCK):
        finish(i)
    for copy in sends:
        copy.wait()


def main(tokens, normed, bias, swapped_far, in_weight, out_weight):
    vmem = pl.BlockSpec(memory_space=pltpu.VMEM)
    updated, _, _ = pl.pallas_call(
        main_kernel,
        out_shape=(
            jax.ShapeDtypeStruct((ROWS, D), jnp.bfloat16),
            jax.ShapeDtypeStruct(in_weight.shape, jnp.bfloat16),
            jax.ShapeDtypeStruct(out_weight.shape, jnp.bfloat16),
        ),
        in_specs=[vmem] * 6,
        out_specs=(pl.BlockSpec(memory_space=pl.ANY), vmem, vmem),
        input_output_aliases={4: 1, 5: 2},
        scratch_shapes=[
            pltpu.VMEM((ROWS, 4 * D), jnp.bfloat16),
            pltpu.VMEM((ROWS, D), jnp.float32),
            pltpu.VMEM((ROWS, D), jnp.bfloat16),
            pltpu.SemaphoreType.DMA((ROWS // BLOCK,)),
        ],
        compiler_params=pltpu.CompilerParams(vmem_limit_bytes=VMEM_MAIN * 2**20),
        cost_estimate=pl.CostEstimate(
            flops=5 * 10**9, bytes_accessed=9 * 10**6, transcendentals=4 * 10**6
        ),
    )(tokens, normed, bias, swapped_far, in_weight, out_weight)
    return updated


def device_of(x, y, z, core):
    return ((z % 8 * 4 + y % 4) * 2 + core % 2) * 4 + x % 4


def moves(step):
    return [
        (device_of(x, y, z, core), device_of(*step(x, y, z, core)))
        for z in range(8)
        for y in range(4)
        for core in range(2)
        for x in range(4)
    ]


def send(array, step):
    return lax.ppermute(array, ("dp", "group"), moves(step))


def gather(in_weight, out_weight):
    part = lax.axis_index("group") * HEAD_DIM

    def piece_of(in_rows, out_rows):
        side = lax.dynamic_slice_in_dim(out_rows, part, HEAD_DIM, axis=1)
        return jnp.concatenate([in_rows, side], axis=1)[None]

    piece = piece_of(in_weight.T, out_weight.T)
    other = piece_of(
        send(in_weight.T, lambda x, y, z, core: (x, y, z ^ 1, core)),
        send(out_weight.T, lambda x, y, z, core: (x, y, z ^ 1, core)),
    )
    unit = jnp.concatenate([piece, other])
    units = [
        unit,
        send(unit, lambda x, y, z, core: (x, y, z + 2 * (z % 2) - 1, core)),
        send(unit, lambda x, y, z, core: (x, y, z + 4 * (z % 2) - 2, core)),
        send(unit, lambda x, y, z, core: (x, y, z + 6 * (z % 2) - 3, core)),
    ]
    line = jnp.concatenate(units)
    lines = [line] + [
        send(line, lambda x, y, z, core, k=k: (x + k * (1 - core), y + k * core, z, core))
        for k in (1, 3, 2)
    ]
    plane = jnp.concatenate(lines)
    return [plane] + [
        send(plane, lambda x, y, z, core, k=k: (x + k * core, y + k * (1 - core), z, core))
        for k in (1, 2, 3)
    ]


def swap(array):
    return send(array, lambda x, y, z, core: (x, y, z, core + 1))


def shards(tokens, stamps, lengths, in_weight, out_weight, pos_table, time_table):
    own_lengths = lengths.reshape(-1)
    planes = gather(in_weight, out_weight)
    swapped_own = swap(planes[0])
    swapped_own, stamps = lax.optimization_barrier((swapped_own, stamps))
    prepared = prepare(own_lengths, pos_table, time_table, tokens, stamps.reshape(8, TILE))
    planes[1], prepared = lax.optimization_barrier((planes[1], prepared))
    planes[2], prepared = lax.optimization_barrier((planes[2], prepared))
    swapped_near = swap(jnp.concatenate([planes[1], planes[3]]))
    return main(*prepared, swap(planes[2]), *arrange(planes, swapped_own, swapped_near))


def solution(mesh):
    return jax.shard_map(
        shards,
        mesh=mesh,
        in_specs=(
            P(("dp", "group"), None),
            P(("dp", "group")),
            P("dp", "group", None),
            P(None, ("dp", "group")),
            P(None, "dp"),
            P(),
            P(),
        ),
        out_specs=P(("dp", "group"), None),
        check_vma=False,
    )
```

```python
import jax
import jax.numpy as jnp
from jax import lax
from jax.experimental import pallas as pl
from jax.experimental.pallas import tpu as pltpu
from jax.sharding import PartitionSpec as P

D = 512
HEADS = 4
HEAD_DIM = 128
ROWS = 1024
BLOCK = 256
TILE = 128
POS_BUCKETS = 12
TIME_BUCKETS = 20
NEVER = -1e30
STEPS = (0, -1, 1, 2, -2, -3, 3, 4)
VMEM_PREPARE = 16
VMEM_MAIN = 32
TRANS_B = (((1,), (1,)), ((), ()))
PAIRS = [(i, j) for i in range(ROWS // BLOCK) for j in range(i + 1)]


def normalize(values):
    center = values - jnp.mean(values, axis=-1, keepdims=True)
    spread = jnp.mean(center * center, axis=-1, keepdims=True)
    return center * lax.rsqrt(spread + 1e-05)


def prepare_kernel(
    lengths_hbm, pos_hbm, time_hbm, tokens_hbm, stamps_hbm, tokens, normed, bias,
    lengths, pos_table, time_table, stamps, pos_tiles, sems,
):
    copies = [
        pltpu.make_async_copy(source, target, sems.at[k])
        for k, (source, target) in enumerate(
            [
                (lengths_hbm, lengths),
                (pos_hbm, pos_table),
                (time_hbm, time_table),
                (stamps_hbm, stamps),
                (tokens_hbm, tokens),
            ]
        )
    ]
    for copy in copies:
        copy.start()
    for copy in copies:
        copy.wait()
    for i in range(ROWS // BLOCK):
        rows = slice(i * BLOCK, (i + 1) * BLOCK)
        normed[rows, :] = normalize(tokens[rows, :].astype(jnp.float32)).astype(jnp.bfloat16)

    apart = lax.broadcasted_iota(jnp.int32, (TILE, TILE), 0) - lax.broadcasted_iota(
        jnp.int32, (TILE, TILE), 1
    )
    for d in range(ROWS // TILE):
        offset = apart + d * TILE
        tile = jnp.full((TILE, TILE), pos_table[0] * 0.5, jnp.float32)
        for power in range(1, POS_BUCKETS):
            if 2**power - 1 <= (d + 1) * TILE - 1:
                tile = jnp.where(offset + 1 >= 2**power, pos_table[power] * 0.5, tile)
        pos_tiles[d] = jnp.where(offset >= 0, tile, NEVER)

    first = lengths[0]
    second = first + lengths[1]
    third = second + lengths[2]
    row_id = (
        lax.broadcasted_iota(jnp.int32, (8, TILE), 0) * TILE
        + lax.broadcasted_iota(jnp.int32, (8, TILE), 1)
    )
    segment = (
        (row_id >= first).astype(jnp.int32)
        + (row_id >= second).astype(jnp.int32)
        + (row_id >= third).astype(jnp.int32)
    )
    times = stamps[...] + segment * (1 << 20)

    lane = lax.broadcasted_iota(jnp.int32, (TILE, TILE), 1)
    lookup = jnp.full((TILE, TILE), NEVER, jnp.float32)
    for entry in range(TIME_BUCKETS):
        lookup = jnp.where(lane == 31 - entry, time_table[entry] * 0.5, lookup)

    for i in range(ROWS // TILE):
        own = jnp.transpose(jnp.broadcast_to(times[i : i + 1, :], (TILE, TILE)))
        own = own + 1
        for j in range(ROWS // TILE):
            qi, kj = i // 2, j // 2
            if kj > qi:
                continue
            at = PAIRS.index((qi, kj))
            rows, cols = pl.ds((i % 2) * TILE, TILE), pl.ds((j % 2) * TILE, TILE)
            if j > i:
                bias[at, rows, cols] = jnp.full((TILE, TILE), NEVER, jnp.float32)
                continue
            gap = own - times[j : j + 1, :]
            time_bias = jnp.take_along_axis(lookup, lax.clz(gap), axis=1)
            bias[at, rows, cols] = time_bias + pos_tiles[i - j]


def prepare(lengths, pos_table, time_table, tokens, stamps):
    hbm = pl.BlockSpec(memory_space=pltpu.HBM)
    vmem = pl.BlockSpec(memory_space=pltpu.VMEM)
    return pl.pallas_call(
        prepare_kernel,
        out_shape=(
            jax.ShapeDtypeStruct((ROWS, D), jnp.bfloat16),
            jax.ShapeDtypeStruct((ROWS, D), jnp.bfloat16),
            jax.ShapeDtypeStruct((len(PAIRS), BLOCK, BLOCK), jnp.float32),
        ),
        in_specs=[hbm] * 5,
        out_specs=(vmem,) * 3,
        scratch_shapes=[
            pltpu.SMEM((4,), jnp.int32),
            pltpu.SMEM((POS_BUCKETS,), jnp.float32),
            pltpu.SMEM((TIME_BUCKETS,), jnp.float32),
            pltpu.VMEM((ROWS // TILE, TILE), jnp.int32),
            pltpu.VMEM((ROWS // TILE, TILE, TILE), jnp.float32),
            pltpu.SemaphoreType.DMA((5,)),
        ],
        compiler_params=pltpu.CompilerParams(vmem_limit_bytes=VMEM_PREPARE * 2**20),
        cost_estimate=pl.CostEstimate(flops=2 * 10**7, bytes_accessed=5 * 10**6, transcendentals=0),
    )(
        *[
            pltpu.with_memory_space_constraint(array, pltpu.HBM)
            for array in (lengths, pos_table, time_table, tokens, stamps)
        ]
    )


def half_silu(z):
    return z + z * jnp.tanh(z)


def line_slot(apart):
    apart = lax.rem(apart, 4)
    slot = jnp.where(apart == 1, 1, jnp.where(apart == 2, 3, 2))
    return jnp.where(apart == 0, 0, slot)


def coordinates():
    dp = lax.axis_index("dp")
    return lax.axis_index("group"), lax.rem(dp // 2, 4), dp // 8, lax.rem(dp, 2)


def place(source, start, own_core, far, in_weight, out_weight):
    own_x, own_y, own_z, core = coordinates()
    core = core if own_core else 1 - core
    step = jnp.where(lax.rem(own_z, 2) == 1, 1, -1)
    first, second = jnp.where(core == 0, own_x, own_y), jnp.where(core == 0, own_y, own_x)
    second = lax.rem(second + 4 - far, 4)

    def line(apart, carry):
        along = lax.rem(first + 4 - apart, 4)
        x, y = jnp.where(core == 0, along, second), jnp.where(core == 0, second, along)
        lanes = pl.ds(pl.multiple_of(x * HEAD_DIM, HEAD_DIM), HEAD_DIM)
        at = start + line_slot(apart) * 8
        for slot in range(8):
            z = lax.rem(own_z + 8 + step * STEPS[slot], 8)
            piece = source[at + slot]
            in_weight[z * 32 + y * 8 + core * 4 + x] = piece[:, :D]
            out_weight[z * 8 + y * 2 + core, :, lanes] = piece[:, D:]
        return carry

    lax.fori_loop(0, 4, line, 0)


def arrange_kernel(own, near, far, last, swapped_own, swapped_near, in_weight, out_weight):
    for k, source in enumerate((own, near, far, last)):
        place(source, 0, True, k, in_weight, out_weight)
    place(swapped_own, 0, False, 0, in_weight, out_weight)
    place(swapped_near, 0, False, 1, in_weight, out_weight)
    place(swapped_near, 32, False, 3, in_weight, out_weight)


def arrange(planes, swapped_own, swapped_near):
    vmem = pl.BlockSpec(memory_space=pltpu.VMEM)
    return pl.pallas_call(
        arrange_kernel,
        out_shape=(
            jax.ShapeDtypeStruct((4 * D // 8, 8, D), jnp.bfloat16),
            jax.ShapeDtypeStruct((D // 8, 8, D), jnp.bfloat16),
        ),
        in_specs=[vmem] * 6,
        out_specs=(vmem,) * 2,
        compiler_params=pltpu.CompilerParams(vmem_limit_bytes=VMEM_PREPARE * 2**20),
        cost_estimate=pl.CostEstimate(flops=10**6, bytes_accessed=10**6, transcendentals=0),
    )(*planes, swapped_own, swapped_near)


def main_kernel(
    tokens, normed, bias, swapped_far, in_weight_given, out_weight_given,
    updated_hbm, in_weight, out_weight, mixed, totals, updated, out_sems,
):
    place(swapped_far, 0, False, 2, in_weight, out_weight)
    for i in range(ROWS // 256):
        rows = pl.ds(i * 256, 256)
        for part in range(4):
            cols = pl.ds(part * 512, 512)
            product = lax.dot_general(
                normed[rows, :], in_weight[pl.ds(part * (D // 8), D // 8)].reshape(D, D), TRANS_B, preferred_element_type=jnp.float32
            )
            mixed[rows, cols] = half_silu(product * 0.5).astype(jnp.bfloat16)
    def finish(at, first, count):
        rows = pl.ds(first, count)
        attended = totals[rows, :].astype(jnp.bfloat16).astype(jnp.float32)
        gate = mixed[rows, pl.ds(0, D)].astype(jnp.float32)
        gated = (normalize(attended) * gate).astype(jnp.bfloat16)
        projected = lax.dot_general(
            gated, out_weight[...].reshape(D, D), TRANS_B, preferred_element_type=jnp.float32
        )
        updated[rows, :] = (tokens[rows, :].astype(jnp.float32) + projected).astype(jnp.bfloat16)
        copy = pltpu.make_async_copy(updated.at[rows, :], updated_hbm.at[rows, :], out_sems.at[at])
        copy.start()
        sends.append(copy)

    sends = []
    for j in range(ROWS // BLOCK):
        rows = pl.ds(j * BLOCK, ROWS - j * BLOCK)
        keys = pl.ds(j * BLOCK, BLOCK)
        pair_bias = jnp.concatenate([bias[PAIRS.index((i, j))] for i in range(j, ROWS // BLOCK)])
        for head in range(HEADS):
            cols = [pl.ds(part * D + head * HEAD_DIM, HEAD_DIM) for part in range(4)]
            scores = lax.dot_general(
                mixed[rows, cols[2]], mixed[keys, cols[3]], TRANS_B,
                preferred_element_type=jnp.float32,
            )
            weights = half_silu(scores * (0.5 * HEAD_DIM**-0.5) + pair_bias).astype(jnp.bfloat16)
            product = jnp.dot(weights, mixed[keys, cols[1]], preferred_element_type=jnp.float32)
            own = pl.ds(head * HEAD_DIM, HEAD_DIM)
            totals[rows, own] = product if j == 0 else totals[rows, own] + product
    for at, (first, count) in enumerate(((0, 512), (512, 256), (768, 256))):
        finish(at, first, count)
    for copy in sends:
        copy.wait()


def main(tokens, normed, bias, swapped_far, in_weight, out_weight):
    vmem = pl.BlockSpec(memory_space=pltpu.VMEM)
    updated, _, _ = pl.pallas_call(
        main_kernel,
        out_shape=(
            jax.ShapeDtypeStruct((ROWS, D), jnp.bfloat16),
            jax.ShapeDtypeStruct(in_weight.shape, jnp.bfloat16),
            jax.ShapeDtypeStruct(out_weight.shape, jnp.bfloat16),
        ),
        in_specs=[vmem] * 6,
        out_specs=(pl.BlockSpec(memory_space=pl.ANY), vmem, vmem),
        input_output_aliases={4: 1, 5: 2},
        scratch_shapes=[
            pltpu.VMEM((ROWS, 4 * D), jnp.bfloat16),
            pltpu.VMEM((ROWS, D), jnp.float32),
            pltpu.VMEM((ROWS, D), jnp.bfloat16),
            pltpu.SemaphoreType.DMA((3,)),
        ],
        compiler_params=pltpu.CompilerParams(vmem_limit_bytes=VMEM_MAIN * 2**20),
        cost_estimate=pl.CostEstimate(
            flops=5 * 10**9, bytes_accessed=9 * 10**6, transcendentals=4 * 10**6
        ),
    )(tokens, normed, bias, swapped_far, in_weight, out_weight)
    return updated


def device_of(x, y, z, core):
    return ((z % 8 * 4 + y % 4) * 2 + core % 2) * 4 + x % 4


def moves(step):
    return [
        (device_of(x, y, z, core), device_of(*step(x, y, z, core)))
        for z in range(8)
        for y in range(4)
        for core in range(2)
        for x in range(4)
    ]


def send(array, step):
    return lax.ppermute(array, ("dp", "group"), moves(step))


def gather(in_weight, out_weight):
    part = lax.axis_index("group") * HEAD_DIM

    def piece_of(in_rows, out_rows):
        side = lax.dynamic_slice_in_dim(out_rows, part, HEAD_DIM, axis=1)
        return jnp.concatenate([in_rows, side], axis=1)[None]

    piece = piece_of(in_weight.T, out_weight.T)
    other = piece_of(
        send(in_weight.T, lambda x, y, z, core: (x, y, z ^ 1, core)),
        send(out_weight.T, lambda x, y, z, core: (x, y, z ^ 1, core)),
    )
    unit = jnp.concatenate([piece, other])
    units = [
        unit,
        send(unit, lambda x, y, z, core: (x, y, z + 2 * (z % 2) - 1, core)),
        send(unit, lambda x, y, z, core: (x, y, z + 4 * (z % 2) - 2, core)),
        send(unit, lambda x, y, z, core: (x, y, z + 6 * (z % 2) - 3, core)),
    ]
    line = jnp.concatenate(units)
    lines = [line] + [
        send(line, lambda x, y, z, core, k=k: (x + k * (1 - core), y + k * core, z, core))
        for k in (1, 3, 2)
    ]
    plane = jnp.concatenate(lines)
    return [plane] + [
        send(plane, lambda x, y, z, core, k=k: (x + k * core, y + k * (1 - core), z, core))
        for k in (1, 2, 3)
    ]


def swap(array):
    return send(array, lambda x, y, z, core: (x, y, z, core + 1))


def shards(tokens, stamps, lengths, in_weight, out_weight, pos_table, time_table):
    own_lengths = lengths.reshape(-1)
    planes = gather(in_weight, out_weight)
    swapped_own = swap(planes[0])
    swapped_own, stamps = lax.optimization_barrier((swapped_own, stamps))
    prepared = prepare(own_lengths, pos_table, time_table, tokens, stamps.reshape(8, TILE))
    planes[1], prepared = lax.optimization_barrier((planes[1], prepared))
    planes[2], prepared = lax.optimization_barrier((planes[2], prepared))
    swapped_near = swap(jnp.concatenate([planes[1], planes[3]]))
    return main(*prepared, swap(planes[2]), *arrange(planes, swapped_own, swapped_near))


def solution(mesh):
    return jax.shard_map(
        shards,
        mesh=mesh,
        in_specs=(
            P(("dp", "group"), None),
            P(("dp", "group")),
            P("dp", "group", None),
            P(None, ("dp", "group")),
            P(None, "dp"),
            P(),
            P(),
        ),
        out_specs=P(("dp", "group"), None),
        check_vma=False,
    )
```
